32 devices in a mesh: exp: 8 (over y, x, core), strip: 4 (over z).
Axes of the slice: x: 2, y: 2, z: 4, core: 2. Of those that a mesh axis runs over, the one named last changes fastest.
Arguments:
- science: float32 [8, 512, 2048], P('exp', 'strip'), may hold values from -30 to 30
- variance: float32 [8, 512, 2048], P('exp', 'strip'), may hold values from 0.25 to 4
- template: float32 [576, 2176], P(None, 'exp'), may hold values from -14 to 14
- offset_rows: int32 [8], P('exp'), may hold values from 0 to 24
- offset_cols: int32 [8], P('exp'), may hold values from 0 to 88
- stamp_rows: int32 [8, 64], P('exp', 'strip'), may hold values from 0 to 96
- stamp_cols: int32 [8, 64], P('exp', 'strip'), may hold values from 0 to 2016
Outputs:
- difference: float32 [8, 512, 2048], P('exp', 'strip')
The draws below stay inside these ranges and needn't reach their ends.
All inputs are finite; a program needn't handle non-finite values.
Results may differ from the reference program's by a relative error of at most 0.0047.
Values sent between devices are 32-bit elements; how exact they have to be, the bound alone decides.
A program may use at most 128 MiB of HBM per device.

```python
import jax
import jax.numpy as jnp
from jax import lax

STRIP_ROWS = 128
COLUMNS = 2048
STAMP_COUNT = 16
STAMP_SIZE = 32
BASES = 27
SPATIAL_TERMS = 6
BACKGROUND_TERMS = 3
SHIFT_MAX_ROWS = 24
KERNEL_HALF = 20
UNKNOWNS = 165
EXPOSURES = 8
IMAGE_ROWS = 512
STAMPS = 64
TEMPLATE_ROWS = 576
TEMPLATE_COLS = 2176
SHIFT_MAX_COLS = 88


def shift_draw(key, stream_id, largest):
    values = jax.random.randint(jax.random.fold_in(key, stream_id), (EXPOSURES,), 0, largest + 1)
    chosen = jax.random.randint(jax.random.fold_in(key, stream_id + 1), (), 0, EXPOSURES)
    second = (chosen + 1 + jax.random.randint(jax.random.fold_in(key, stream_id + 2), (), 0, EXPOSURES - 1)) % EXPOSURES
    places = jnp.arange(EXPOSURES)
    values = jnp.where(places == chosen, largest, values)
    values = jnp.where(places == second, 0, values)
    return values.astype(jnp.int32)


def template_draw(key):
    shape_all = (TEMPLATE_ROWS, TEMPLATE_COLS)
    scales = 2.0 * jnp.exp(jax.random.uniform(jax.random.fold_in(key, 3001), shape_all, jnp.float32, -0.5, 0.5))
    rough_part = jax.random.truncated_normal(jax.random.fold_in(key, 3003), -4.0, 4.0, shape_all, jnp.float32)
    return scales * rough_part


def variance_draw(key):
    shape_all = (EXPOSURES, IMAGE_ROWS, COLUMNS)
    return jnp.exp(jax.random.uniform(jax.random.fold_in(key, 5003), shape_all, jnp.float32, -1.3862944, 1.3862944))


def draw_template(key, part):
    return template_draw(key)


def draw_variance(key, part):
    return variance_draw(key)


def draw_offset_rows(key, part):
    return shift_draw(key, 1000, SHIFT_MAX_ROWS)


def draw_offset_cols(key, part):
    return shift_draw(key, 2000, SHIFT_MAX_COLS)


def draw_science(key, part):
    template = template_draw(key)
    variance = variance_draw(key)
    shift_down = shift_draw(key, 1000, SHIFT_MAX_ROWS)
    shift_side = shift_draw(key, 2000, SHIFT_MAX_COLS)
    kernel_grid = jnp.arange(3, dtype=jnp.float32) - 1.0
    radius = kernel_grid[:, None] ** 2 + kernel_grid[None, :] ** 2
    jitter = jax.random.normal(jax.random.fold_in(key, 4001), (EXPOSURES, 3, 3), jnp.float32)
    kernels = jnp.exp(-radius / 1.28)[None] * jnp.exp(0.4 * jitter)
    kernels = kernels / jnp.sum(kernels, axis=(1, 2), keepdims=True)
    tilt_terms = jax.random.uniform(jax.random.fold_in(key, 4002), (EXPOSURES, 2), jnp.float32, -0.3, 0.3)
    levels = jax.random.uniform(jax.random.fold_in(key, 4003), (EXPOSURES, 3), jnp.float32, -1.0, 1.0)
    shape_all = (EXPOSURES, IMAGE_ROWS, COLUMNS)
    noise_draw = jax.random.truncated_normal(jax.random.fold_in(key, 4005), -4.0, 4.0, shape_all, jnp.float32)
    side_pos = (2.0 * jnp.arange(COLUMNS, dtype=jnp.float32) + 1.0 - COLUMNS) / COLUMNS
    down_pos = (2.0 * jnp.arange(IMAGE_ROWS, dtype=jnp.float32) + 1.0 - IMAGE_ROWS) / IMAGE_ROWS

    def one_exposure(inputs):
        down_shift, side_shift, kernel, tilt_pair, level_terms, noise_var, noise_value = inputs
        window = lax.dynamic_slice(template, (down_shift + KERNEL_HALF - 1, side_shift + KERNEL_HALF - 1), (IMAGE_ROWS + 2, COLUMNS + 2))
        signal = jnp.zeros((IMAGE_ROWS, COLUMNS), jnp.float32)
        for i in range(3):
            for j in range(3):
                signal = signal + kernel[i, j] * window[i:i + IMAGE_ROWS, j:j + COLUMNS]
        signal = signal * (1.0 + tilt_pair[0] * side_pos[None, :] + tilt_pair[1] * down_pos[:, None])
        signal = signal + level_terms[0] + level_terms[1] * side_pos[None, :] + level_terms[2] * down_pos[:, None]
        return signal + jnp.sqrt(noise_var) * noise_value
    return lax.map(one_exposure, (shift_down, shift_side, kernels, tilt_terms, levels, variance, noise_draw))


def touch_ends(values, own_key, low, top_value):
    shape = values.shape
    index_at = [jax.random.randint(jax.random.fold_in(own_key, axis), (), 0, shape[axis]) for axis in range(len(shape))]
    values = values.at[tuple(index_at)].set(low)
    longest = shape.index(max(shape))
    index_at[longest] = (index_at[longest] + 1) % shape[longest]
    return values.at[tuple(index_at)].set(top_value)


def setup_inputs(seed: int = 0) -> dict:
    seeds = jax.random.split(jax.random.key(seed), 8)
    return {
        "science": draw_science(jax.random.fold_in(seeds[7], 71), 0),
        "variance": draw_variance(jax.random.fold_in(seeds[7], 71), 0),
        "template": draw_template(jax.random.fold_in(seeds[7], 71), 0),
        "offset_rows": draw_offset_rows(jax.random.fold_in(seeds[7], 71), 0),
        "offset_cols": draw_offset_cols(jax.random.fold_in(seeds[7], 71), 0),
        "stamp_rows": touch_ends(jax.random.randint(seeds[5], (EXPOSURES, STAMPS), 0, STRIP_ROWS - STAMP_SIZE + 1), jax.random.fold_in(seeds[5], 1), 0, STRIP_ROWS - STAMP_SIZE).astype(jnp.int32),
        "stamp_cols": touch_ends(jax.random.randint(seeds[6], (EXPOSURES, STAMPS), 0, COLUMNS - STAMP_SIZE + 1), jax.random.fold_in(seeds[6], 1), 0, COLUMNS - STAMP_SIZE).astype(jnp.int32),
    }


SIGMAS = (1.0, 2.0, 4.0)
DEGREES = (4, 2, 2)
RIDGE = 0.001

def filter_table(half_width):
    offsets = jnp.arange(-half_width, half_width + 1).astype(jnp.float32)
    entries = []
    for spread, degree in zip(SIGMAS, DEGREES):
        profile = jnp.exp(-offsets * offsets / (2.0 * spread * spread))
        profile = profile / jnp.sum(profile)
        scaled = offsets / spread
        for exponent in range(degree + 1):
            power = jnp.ones_like(scaled)
            for step in range(exponent):
                power = power * scaled
            entries.append(power * profile)
    return jnp.stack(entries)

def filter_groups():
    groups_list = []
    first_filter = 0
    basis_number = 0
    for degree in DEGREES:
        members_by = [[] for b in range(degree + 1)]
        for across in range(degree + 1):
            for downward in range(degree + 1 - across):
                members_by[downward].append((basis_number, first_filter + across))
                basis_number += 1
        for downward in range(degree + 1):
            groups_list.append((first_filter + downward, members_by[downward]))
        first_filter += degree + 1
    return groups_list

def band_matrix(tap_table, block_size):
    tap_count = tap_table.shape[1]
    distance = jnp.arange(block_size + tap_count - 1)[:, None] - jnp.arange(block_size)[None, :]
    onehot = (jnp.arange(tap_count)[:, None, None] == distance[None]).astype(jnp.float32)
    return jnp.einsum('ft,tjc->fjc', tap_table.astype(jnp.float32), onehot, precision=lax.Precision.HIGHEST)

def filter_down(picture, tap_table, out_rows):
    tap_count = tap_table.shape[1]
    block_size = min(128, out_rows)
    banded = band_matrix(tap_table, block_size)
    slab_stack = jnp.stack([picture[i * block_size:i * block_size + block_size + tap_count - 1] for i in range(out_rows // block_size)], 0)
    result = jnp.einsum('njc,fjr->fnrc', slab_stack.astype(jnp.float32), banded.astype(jnp.float32), precision=lax.Precision.HIGHEST, preferred_element_type=jnp.float32)
    return result.reshape(tap_table.shape[0], out_rows, picture.shape[1])

def filter_across(picture, tap_table, out_cols):
    tap_count = tap_table.shape[1]
    block_size = min(128, out_cols)
    banded = band_matrix(tap_table, block_size)
    slab_stack = jnp.stack([picture[..., i * block_size:i * block_size + block_size + tap_count - 1] for i in range(out_cols // block_size)], -2)
    result = jnp.einsum('...nj,fjc->f...nc', slab_stack.astype(jnp.float32), banded.astype(jnp.float32), precision=lax.Precision.HIGHEST, preferred_element_type=jnp.float32)
    return result.reshape(result.shape[:-2] + (out_cols,))

def spatial_terms(across, downward):
    all_ones = jnp.ones_like(across * downward)
    return [all_ones, across * all_ones, downward * all_ones, across * across * all_ones, across * downward, downward * downward * all_ones]

def ridge_solve(normal, right_side):
    unknowns = normal.shape[0]
    ridge_value = RIDGE * jnp.trace(normal) / unknowns
    factor = jnp.linalg.cholesky(normal + ridge_value * jnp.eye(unknowns, dtype=normal.dtype))
    middle = lax.linalg.triangular_solve(factor, right_side[:, None], left_side=True, lower=True)
    result = lax.linalg.triangular_solve(factor, middle, left_side=True, lower=True, transpose_a=True)
    return result[:, 0]

def stamp_design(vertical, picture, noise_var, top_rows, left_cols, row_base, image_rows, short_taps, groups_list):
    filters = vertical.shape[0]
    inside = jnp.arange(STAMP_SIZE)

    def cut_filtered(top_row, left_col):
        anchor = jnp.zeros((), jnp.int32)
        return lax.dynamic_slice(vertical, (anchor, top_row, left_col), (filters, STAMP_SIZE, STAMP_SIZE + 2 * KERNEL_HALF))

    def cut_plain(source, top_row, left_col):
        return lax.dynamic_slice(source, (top_row, left_col), (STAMP_SIZE, STAMP_SIZE))
    cutouts = jax.vmap(cut_filtered)(top_rows, left_cols)
    sci_stamps = jax.vmap(cut_plain, (None, 0, 0))(picture, top_rows, left_cols)
    var_stamps = jax.vmap(cut_plain, (None, 0, 0))(noise_var, top_rows, left_cols)
    basis_list = [None] * BASES
    for index_down, members in groups_list:
        filtered = filter_across(cutouts[:, index_down], short_taps[members[0][1]:members[-1][1] + 1], STAMP_SIZE)
        for position, member in enumerate(members):
            basis_list[member[0]] = filtered[position]
    pixel_rows = (row_base + top_rows[:, None, None] + inside[None, :, None]).astype(jnp.float32)
    pixel_cols = (left_cols[:, None, None] + inside[None, None, :]).astype(jnp.float32)
    across = (2.0 * pixel_cols + 1.0 - COLUMNS) / COLUMNS
    downward = (2.0 * pixel_rows + 1.0 - image_rows) / image_rows
    term_list = spatial_terms(across, downward)
    columns_list = []
    for basis_number in range(BASES):
        for spatial in term_list:
            columns_list.append(spatial * basis_list[basis_number])
    for spatial in term_list[:BACKGROUND_TERMS]:
        columns_list.append(spatial)
    design = jnp.stack(columns_list).reshape(UNKNOWNS, -1)
    weights = (1.0 / var_stamps).reshape(-1)
    weighted = design * weights[None, :]
    normal = jnp.dot(weighted.astype(jnp.float32), design.T.astype(jnp.float32), precision=lax.Precision.HIGHEST, preferred_element_type=jnp.float32)
    right_side = jnp.dot(weighted.astype(jnp.float32), sci_stamps.reshape(-1).astype(jnp.float32), precision=lax.Precision.HIGHEST, preferred_element_type=jnp.float32)
    return (normal, right_side)

def model_image(vertical_cols, coefficients, full_terms, short_taps, groups_list, out_cols):
    offset_bg = SPATIAL_TERMS * BASES
    predicted = coefficients[offset_bg] * full_terms[0]
    for i in range(1, BACKGROUND_TERMS):
        predicted = predicted + coefficients[offset_bg + i] * full_terms[i]
    for index_down, members in groups_list:
        filtered = filter_across(vertical_cols[index_down], short_taps[members[0][1]:members[-1][1] + 1], out_cols)
        for position, member in enumerate(members):
            basis_number = member[0]
            spatial_field = coefficients[SPATIAL_TERMS * basis_number] * full_terms[0]
            for j in range(1, SPATIAL_TERMS):
                spatial_field = spatial_field + coefficients[SPATIAL_TERMS * basis_number + j] * full_terms[j]
            predicted = predicted + spatial_field * filtered[position]
    return predicted

def reference(science, variance, template, offset_rows, offset_cols, stamp_rows, stamp_cols):
    tap_table = filter_table(KERNEL_HALF).astype(jnp.float32)
    short_taps = tap_table.astype(jnp.bfloat16)
    groups_list = filter_groups()
    column_pos = (2.0 * jnp.arange(COLUMNS, dtype=jnp.float32) + 1.0 - COLUMNS) / COLUMNS
    row_pos = (2.0 * jnp.arange(IMAGE_ROWS, dtype=jnp.float32) + 1.0 - IMAGE_ROWS) / IMAGE_ROWS
    full_terms = spatial_terms(column_pos[None, :], row_pos[:, None])
    strip_start = (jnp.arange(STAMPS) // STAMP_COUNT * STRIP_ROWS).astype(jnp.int32)

    def one_exposure(inputs):
        picture, noise_var, shift_down, shift_side, corner_down, corner_side = inputs
        window = lax.dynamic_slice(template, (shift_down.astype(jnp.int32), shift_side.astype(jnp.int32)), (IMAGE_ROWS + 2 * KERNEL_HALF, COLUMNS + 2 * KERNEL_HALF))
        vertical = filter_down(window, tap_table, IMAGE_ROWS).astype(jnp.bfloat16)
        top_rows = (strip_start + corner_down.astype(jnp.int32)).astype(jnp.int32)
        left_cols = corner_side.astype(jnp.int32)
        normal, right_side = stamp_design(vertical, picture, noise_var, top_rows, left_cols, jnp.zeros((), jnp.int32), IMAGE_ROWS, short_taps, groups_list)
        coefficients = ridge_solve(normal, right_side)
        predicted = model_image(vertical, coefficients, full_terms, short_taps, groups_list, COLUMNS)
        return picture - predicted
    return lax.map(one_exposure, (science, variance, offset_rows, offset_cols, stamp_rows, stamp_cols))
```

```python
import functools

import jax
import jax.numpy as jnp
import ml_dtypes
import numpy as np
from jax import lax
from jax.experimental import pallas as pl
from jax.experimental.pallas import tpu as pltpu
from jax.sharding import PartitionSpec as P

STAMP_SIZE = 32
STAMP_COUNT = 16
BASES = 27
SPATIAL_TERMS = 6
BACKGROUND_TERMS = 3
KERNEL_HALF = 20
TAPS = 2 * KERNEL_HALF + 1
UNKNOWNS = 165
SHIFT_MAX_ROWS = 24

SIGMAS = (1.0, 2.0, 4.0)
DEGREES = (4, 2, 2)
RIDGE = 0.001

SLOT = 32
SYSTEM = SLOT * SPATIAL_TERMS
FILTERS = 11
GROUP = 4
BF16 = ml_dtypes.bfloat16


def filter_table():
    offsets = np.arange(-KERNEL_HALF, KERNEL_HALF + 1).astype(np.float64)
    entries = []
    for spread, degree in zip(SIGMAS, DEGREES):
        profile = np.exp(-offsets * offsets / (2.0 * spread * spread))
        profile = profile / np.sum(profile)
        for exponent in range(degree + 1):
            entries.append((offsets / spread) ** exponent * profile)
    return np.stack(entries).astype(np.float32)


def filter_groups():
    groups = []
    first_filter = 0
    basis = 0
    for gaussian, degree in enumerate(DEGREES):
        members = [[] for _ in range(degree + 1)]
        for across in range(degree + 1):
            for down in range(degree + 1 - across):
                members[down].append((basis, across))
                basis += 1
        for down in range(degree + 1):
            groups.append((first_filter + down, gaussian, members[down]))
        first_filter += degree + 1
    return groups


def split_band(table, out_rows, in_rows, depth):
    band = np.zeros((table.shape[0], out_rows, in_rows), np.float32)
    for r in range(out_rows):
        band[:, r, r : r + TAPS] = table
    high = band.astype(BF16)
    low = (band - high.astype(np.float32)).astype(BF16)
    full = np.zeros((table.shape[0], out_rows, depth), BF16)
    full[:, :, 0:in_rows] = high
    full[:, :, in_rows : 2 * in_rows] = high
    full[:, :, 2 * in_rows : 3 * in_rows] = low
    return full.reshape(table.shape[0] * out_rows, depth)


def stamp_bands(table):
    result = []
    first = 0
    for degree in DEGREES:
        band = np.zeros((GROUP * 128, (degree + 1) * 128), np.float32)
        for a in range(degree + 1):
            for s in range(GROUP):
                for c in range(STAMP_SIZE):
                    band[s * 128 + c : s * 128 + c + TAPS, a * 128 + s * 32 + c] = table[first + a]
        result.append(band.astype(BF16))
        first += degree + 1
    return result


def across_bands(table):
    result = []
    first = 0
    for degree in DEGREES:
        band = np.zeros((256, (degree + 1) * 128), np.float32)
        for a in range(degree + 1):
            for c in range(128):
                band[c : c + TAPS, a * 128 + c] = table[first + a]
        result.append(band.astype(BF16))
        first += degree + 1
    return result


def split(value):
    high = value.astype(jnp.bfloat16)
    low = (value - high.astype(jnp.float32)).astype(jnp.bfloat16)
    return high, low


def cut(source, top, tile, height):
    read = height + 8
    first = jnp.minimum(top // 8, (source.shape[0] - read) // 8) * 8
    block = source[
        pl.ds(pl.multiple_of(first, 8), read), pl.ds(pl.multiple_of(tile * 128, 128), 256)
    ]
    return pltpu.roll(block, lax.rem(read - (top - first), read), 0)[:height]


def stamp_kernel(
    image_rows, columns, place, rows, cols, win, sci, var, vband, h0, h1, h2,
    out, patch, vert, basis, weight, dhigh, dlow,
):
    shift_down, shift_side, row_base = place[0], place[1], place[2]
    win_tiles = win.shape[1] // 128
    sci_tiles = columns // 128
    bands = (h0, h1, h2)
    pad = jnp.zeros((8, 128), jnp.float32)
    lane = lax.broadcasted_iota(jnp.int32, (STAMP_SIZE, 128), 1)
    for g in range(STAMP_COUNT // GROUP):
        sci_group = jnp.zeros((STAMP_SIZE, 128), jnp.float32)
        var_group = jnp.ones((STAMP_SIZE, 128), jnp.float32)
        for i in range(GROUP):
            s = g * GROUP + i
            top, left = rows[s], cols[s]
            start = shift_side + left
            tile = jnp.minimum(start // 128, win_tiles - 2)
            shift = start - tile * 128
            piece = cut(win, shift_down + top, tile, 72)
            piece = pltpu.roll(piece, lax.rem(256 - shift, 256), 1)[:, :128]
            piece = jnp.concatenate([piece, pad], 0)
            high, low = split(piece)
            patch[:, i * 128 : (i + 1) * 128] = jnp.concatenate(
                [high, low, high, jnp.zeros((16, 128), jnp.bfloat16)], 0
            )
            tile = jnp.minimum(left // 128, sci_tiles - 2)
            shift = lax.rem(256 + i * STAMP_SIZE - (left - tile * 128), 256)
            inside = (lane >= i * STAMP_SIZE) & (lane < (i + 1) * STAMP_SIZE)
            sci_group = jnp.where(inside, pltpu.roll(cut(sci, top, tile, STAMP_SIZE), shift, 1)[:, :128], sci_group)
            var_group = jnp.where(inside, pltpu.roll(cut(var, top, tile, STAMP_SIZE), shift, 1)[:, :128], var_group)
        span = slice(g * STAMP_SIZE, (g + 1) * STAMP_SIZE)
        weight[span, :] = 1.0 / jnp.sqrt(var_group)
        basis[28 * 128 + g * STAMP_SIZE : 28 * 128 + (g + 1) * STAMP_SIZE, :] = sci_group
        filtered = jnp.dot(vband[...], patch[...], preferred_element_type=jnp.float32)
        for m in range(FILTERS):
            vert[m * 128 + g * 32 : m * 128 + g * 32 + 32, :] = filtered[
                m * 32 : m * 32 + 32
            ].astype(jnp.bfloat16)
    basis[27 * 128 : 28 * 128, :] = jnp.ones((128, 128), jnp.float32)
    basis[29 * 128 :, :] = jnp.zeros((3 * 128, 128), jnp.float32)
    for m, gaussian, members in filter_groups():
        width = len(members) * 128
        result = jnp.dot(
            vert[m * 128 : (m + 1) * 128, :],
            bands[gaussian][:, :width],
            preferred_element_type=jnp.float32,
        )
        for k, a in members:
            basis[k * 128 : (k + 1) * 128, :] = result[:, a * 128 : (a + 1) * 128]

    lane_row = lax.broadcasted_iota(jnp.int32, (1, 128), 1)
    total = jnp.zeros((SYSTEM, SYSTEM), jnp.float32)
    contract = (((1,), (1,)), ((), ()))
    for g in range(STAMP_COUNT // GROUP):
        tops = jnp.zeros((1, 128), jnp.int32)
        lefts = jnp.zeros((1, 128), jnp.int32)
        for i in range(GROUP):
            inside = (lane_row >= i * STAMP_SIZE) & (lane_row < (i + 1) * STAMP_SIZE)
            tops = jnp.where(inside, rows[g * GROUP + i], tops)
            lefts = jnp.where(inside, cols[g * GROUP + i] - i * STAMP_SIZE, lefts)
        x = (2.0 * (lefts + lane_row).astype(jnp.float32) + 1.0 - columns) / columns
        tops = tops + row_base

        def one_row(r, carry):
            at = g * STAMP_SIZE + r
            y = (2.0 * (tops + r).astype(jnp.float32) + 1.0 - image_rows) / image_rows
            images = basis[pl.ds(at, SLOT, stride=128), :]
            images = images * weight[pl.ds(at, 1), :]
            place_at = pl.ds(pl.multiple_of(r * 128, 128), 128)
            for j, term in enumerate((None, x, y, x * x, x * y, y * y)):
                high, low = split(images if term is None else images * term)
                dhigh[j * SLOT : (j + 1) * SLOT, place_at] = high
                dlow[j * SLOT : (j + 1) * SLOT, place_at] = low
            return carry

        lax.fori_loop(0, STAMP_SIZE, one_row, 0, unroll=4)
        high, low = dhigh[...], dlow[...]
        total += lax.dot_general(high, high, contract, preferred_element_type=jnp.float32)
        total += lax.dot_general(high, low, contract, preferred_element_type=jnp.float32)
        total += lax.dot_general(low, high, contract, preferred_element_type=jnp.float32)
    out[...] = total


def is_unknown(j, k):
    return k < BASES or (k == BASES and j < BACKGROUND_TERMS)


def solve_kernel(normal, out):
    row = lax.broadcasted_iota(jnp.int32, (SYSTEM, SYSTEM), 0)
    col = lax.broadcasted_iota(jnp.int32, (SYSTEM, SYSTEM), 1)
    slot = row % SLOT
    used = (slot < BASES) | ((slot == BASES) & (row < SLOT * BACKGROUND_TERMS))
    system = jnp.where(used, normal[...], 0.0)
    diagonal = used & (row == col)
    trace = jnp.sum(jnp.where(diagonal, system, 0.0), axis=(0, 1), keepdims=True)
    system = system + jnp.where(diagonal, RIDGE * trace / UNKNOWNS, 0.0)
    local = lax.broadcasted_iota(jnp.int32, (SLOT, 1), 0)
    panels = []
    for j in range(SPATIAL_TERMS):
        panel = system[:SLOT]
        for k in range(SLOT):
            if not is_unknown(j, k):
                continue
            at = j * SLOT + k
            pivot_row = panel[k : k + 1] * (1.0 / panel[k : k + 1, at : at + 1])
            panel = jnp.where(local == k, pivot_row, panel - panel[:, at : at + 1] * pivot_row)
        panels.append(panel)
        if j < SPATIAL_TERMS - 1:
            below = system[SLOT:]
            system = below - jnp.dot(
                below[:, j * SLOT : (j + 1) * SLOT],
                panel,
                precision=lax.Precision.HIGHEST,
                preferred_element_type=jnp.float32,
            )
    solved = [None] * SPATIAL_TERMS
    for j in reversed(range(SPATIAL_TERMS)):
        value = panels[j][:, :128]
        for later in range(j + 1, SPATIAL_TERMS):
            value = value - jnp.dot(
                panels[j][:, later * SLOT : (later + 1) * SLOT],
                solved[later],
                precision=lax.Precision.HIGHEST,
                preferred_element_type=jnp.float32,
            )
        solved[j] = value
        out[j * SLOT : (j + 1) * SLOT, :] = value


def vertical_kernel(window, band, out):
    out[...] = jnp.dot(band[...], window[...], preferred_element_type=jnp.float32).astype(
        jnp.bfloat16
    )


def model_kernel(image_rows, columns, place, coef, sci, left, right, h0, h1, h2, out, ya, yb):
    bands = (h0, h1, h2)
    tile = pl.program_id(0)
    shape = sci.shape
    rows = lax.broadcasted_iota(jnp.int32, shape, 0) + place[2]
    y = (2.0 * rows.astype(jnp.float32) + 1.0 - image_rows) / image_rows
    cols = lax.broadcasted_iota(jnp.int32, (1, 128), 1) + tile * 128
    x = (2.0 * cols.astype(jnp.float32) + 1.0 - columns) / columns

    @pl.when(tile == 0)
    def _():
        for k in range(BASES):
            ya[k] = coef[k] + y * (coef[2 * SLOT + k] + y * coef[5 * SLOT + k])
            yb[k] = coef[SLOT + k] + y * coef[4 * SLOT + k]

    total = sci[...] - (coef[BASES] + coef[SLOT + BASES] * x + coef[2 * SLOT + BASES] * y)
    for m, gaussian, members in filter_groups():
        at = slice(m * shape[0], (m + 1) * shape[0])
        picture = jnp.concatenate([left[at, :], right[at, :]], 1)
        result = jnp.dot(
            picture, bands[gaussian][:, : len(members) * 128], preferred_element_type=jnp.float32
        )
        for k, a in members:
            field = ya[k] + x * (yb[k] + x * coef[3 * SLOT + k])
            total = total - field * result[:, a * 128 : (a + 1) * 128]
    out[...] = total


def shards(science, variance, template, offset_rows, offset_cols, stamp_rows, stamp_cols):
    strip_rows = science.shape[1]
    columns = science.shape[2]
    strip_count = lax.axis_size("strip")
    strip_index = lax.axis_index("strip")
    image_rows = strip_rows * strip_count
    window_rows = strip_rows + 2 * KERNEL_HALF
    table = filter_table()
    short = table.astype(BF16).astype(np.float32)
    row_base = strip_index * strip_rows
    own = lax.dynamic_slice_in_dim(template, row_base, window_rows + SHIFT_MAX_ROWS, 0)
    strip = lax.all_gather(own, "exp", axis=1, tiled=True)
    place = jnp.stack([offset_rows[0], offset_cols[0], row_base.astype(jnp.int32)])
    science = science[0]
    variance = variance[0]
    smem = pl.BlockSpec(memory_space=pltpu.SMEM)
    vmem = pl.BlockSpec(memory_space=pltpu.VMEM)
    limit = pltpu.CompilerParams(vmem_limit_bytes=56 * 1024 * 1024)
    across = [jnp.asarray(b) for b in across_bands(short)]

    normal = pl.pallas_call(
        functools.partial(stamp_kernel, image_rows, columns),
        out_shape=jax.ShapeDtypeStruct((SYSTEM, SYSTEM), jnp.float32),
        in_specs=[smem] * 3 + [vmem] * 7,
        out_specs=vmem,
        scratch_shapes=[
            pltpu.VMEM((256, GROUP * 128), jnp.bfloat16),
            pltpu.VMEM((FILTERS * 128, GROUP * 128), jnp.bfloat16),
            pltpu.VMEM((SLOT * 128, 128), jnp.float32),
            pltpu.VMEM((128, 128), jnp.float32),
            pltpu.VMEM((SYSTEM, STAMP_SIZE * 128), jnp.bfloat16),
            pltpu.VMEM((SYSTEM, STAMP_SIZE * 128), jnp.bfloat16),
        ],
        compiler_params=limit,
        name="stamp_sums",
    )(
        place,
        stamp_rows[0],
        stamp_cols[0],
        strip,
        science,
        variance,
        jnp.asarray(split_band(table, STAMP_SIZE, 80, 256)),
        *[jnp.asarray(b) for b in stamp_bands(short)],
    )
    normal = lax.psum(normal, "strip")

    wide = -(-(columns + 128) // 256) * 256
    window = lax.dynamic_slice(
        strip, (offset_rows[0], offset_cols[0]), (window_rows, columns + 2 * KERNEL_HALF)
    )
    window = jnp.pad(window, ((0, 0), (0, wide - window.shape[1])))
    high, low = split(window)
    depth = -(-3 * window_rows // 256) * 256
    filler = jnp.zeros((depth - 3 * window_rows, wide), jnp.bfloat16)
    vertical = pl.pallas_call(
        vertical_kernel,
        grid=(wide // 256,),
        out_shape=jax.ShapeDtypeStruct((FILTERS * strip_rows, wide), jnp.bfloat16),
        in_specs=[
            pl.BlockSpec((depth, 256), lambda i: (0, i)),
            pl.BlockSpec((FILTERS * strip_rows, depth), lambda i: (0, 0)),
        ],
        out_specs=pl.BlockSpec((FILTERS * strip_rows, 256), lambda i: (0, i)),
        cost_estimate=pl.CostEstimate(
            flops=2 * FILTERS * strip_rows * depth * wide,
            bytes_accessed=FILTERS * strip_rows * wide * 2,
            transcendentals=0,
        ),
        compiler_params=limit,
        name="vertical",
    )(
        jnp.concatenate([high, low, high, filler], 0),
        jnp.asarray(split_band(table, strip_rows, window_rows, depth)),
    )

    solved = pl.pallas_call(
        solve_kernel,
        out_shape=jax.ShapeDtypeStruct((SYSTEM, 128), jnp.float32),
        in_specs=[vmem],
        out_specs=vmem,
        compiler_params=limit,
        name="solve",
    )(normal)
    coefficients = solved[:, BASES + 1]

    rows_all = FILTERS * strip_rows
    difference = pl.pallas_call(
        functools.partial(model_kernel, image_rows, columns),
        grid=(columns // 128,),
        out_shape=jax.ShapeDtypeStruct((strip_rows, columns), jnp.float32),
        in_specs=[
            smem,
            smem,
            pl.BlockSpec((strip_rows, 128), lambda i: (0, i)),
            pl.BlockSpec((rows_all, 128), lambda i: (0, i)),
            pl.BlockSpec((rows_all, 128), lambda i: (0, i + 1)),
        ]
        + [pl.BlockSpec(b.shape, lambda i: (0, 0)) for b in across],
        out_specs=pl.BlockSpec((strip_rows, 128), lambda i: (0, i)),
        scratch_shapes=[
            pltpu.VMEM((BASES, strip_rows, 128), jnp.float32),
            pltpu.VMEM((BASES, strip_rows, 128), jnp.float32),
        ],
        compiler_params=limit,
        name="model",
    )(place, coefficients, science, vertical, vertical, *across)
    return difference[None]


def solution(mesh):
    in_specs = (
        P("exp", "strip", None),
        P("exp", "strip", None),
        P(None, "exp"),
        P("exp"),
        P("exp"),
        P("exp", "strip"),
        P("exp", "strip"),
    )
    out_specs = P("exp", "strip", None)
    return jax.shard_map(shards, mesh=mesh, in_specs=in_specs, out_specs=out_specs, check_vma=False)
```

```python
import functools

import jax
import jax.numpy as jnp
import ml_dtypes
import numpy as np
from jax import lax
from jax.experimental import pallas as pl
from jax.experimental.pallas import tpu as pltpu
from jax.sharding import PartitionSpec as P

STAMP_SIZE = 32
STAMP_COUNT = 16
BASES = 27
SPATIAL_TERMS = 6
BACKGROUND_TERMS = 3
KERNEL_HALF = 20
TAPS = 2 * KERNEL_HALF + 1
UNKNOWNS = 165
SHIFT_MAX_ROWS = 24

SIGMAS = (1.0, 2.0, 4.0)
DEGREES = (4, 2, 2)
RIDGE = 0.001

SLOT = 32
SYSTEM = SLOT * SPATIAL_TERMS
FILTERS = 11
PACKED = SYSTEM + SYSTEM - 128
GROUP = 4
MODEL_TILES = 4
MESH = pl.DeviceIdType.MESH
BF16 = ml_dtypes.bfloat16


def filter_table():
    offsets = np.arange(-KERNEL_HALF, KERNEL_HALF + 1).astype(np.float64)
    entries = []
    for spread, degree in zip(SIGMAS, DEGREES):
        profile = np.exp(-offsets * offsets / (2.0 * spread * spread))
        profile = profile / np.sum(profile)
        for exponent in range(degree + 1):
            entries.append((offsets / spread) ** exponent * profile)
    return np.stack(entries).astype(np.float32)


def filter_groups():
    groups = []
    first_filter = 0
    basis = 0
    for gaussian, degree in enumerate(DEGREES):
        members = [[] for _ in range(degree + 1)]
        for across in range(degree + 1):
            for down in range(degree + 1 - across):
                members[down].append((basis, across))
                basis += 1
        for down in range(degree + 1):
            groups.append((first_filter + down, gaussian, members[down]))
        first_filter += degree + 1
    return groups


def split_band(table, out_rows, in_rows, depth):
    band = np.zeros((table.shape[0], out_rows, in_rows), np.float32)
    for r in range(out_rows):
        band[:, r, r : r + TAPS] = table
    high = band.astype(BF16)
    low = (band - high.astype(np.float32)).astype(BF16)
    full = np.zeros((table.shape[0], out_rows, depth), BF16)
    full[:, :, 0:in_rows] = high
    full[:, :, in_rows : 2 * in_rows] = high
    full[:, :, 2 * in_rows : 3 * in_rows] = low
    return full.reshape(table.shape[0] * out_rows, depth)


def stamp_bands(table):
    result = []
    first = 0
    for degree in DEGREES:
        band = np.zeros((GROUP * 128, (degree + 1) * 128), np.float32)
        for a in range(degree + 1):
            for s in range(GROUP):
                for c in range(STAMP_SIZE):
                    band[s * 128 + c : s * 128 + c + TAPS, a * 128 + s * 32 + c] = table[first + a]
        result.append(band.astype(BF16))
        first += degree + 1
    return result


def across_bands(table):
    result = []
    first = 0
    for degree in DEGREES:
        band = np.zeros((256, (degree + 1) * 128), np.float32)
        for a in range(degree + 1):
            for c in range(128):
                band[c : c + TAPS, a * 128 + c] = table[first + a]
        result.append(band.astype(BF16))
        first += degree + 1
    return result


def split(value):
    high = value.astype(jnp.bfloat16)
    low = (value - high.astype(jnp.float32)).astype(jnp.bfloat16)
    return high, low


def cut(source, top, tile, height):
    read = height + 8
    first = jnp.minimum(top // 8, (source.shape[0] - read) // 8) * 8
    block = source[
        pl.ds(pl.multiple_of(first, 8), read), pl.ds(pl.multiple_of(tile * 128, 128), 256)
    ]
    return pltpu.roll(block, lax.rem(read - (top - first), read), 0)[:height]


def stamp_kernel(
    image_rows, columns, place, rows, cols, win, sci, var, vband, h0, h1, h2,
    out, patch, vert, basis, weight, design,
):
    shift_down, shift_side, row_base = place[0], place[1], place[2]
    win_tiles = win.shape[1] // 128
    sci_tiles = columns // 128
    bands = (h0, h1, h2)
    pad = jnp.zeros((8, 128), jnp.float32)
    lane = lax.broadcasted_iota(jnp.int32, (STAMP_SIZE, 128), 1)
    for g in range(STAMP_COUNT // GROUP):
        sci_group = jnp.zeros((STAMP_SIZE, 128), jnp.float32)
        var_group = jnp.ones((STAMP_SIZE, 128), jnp.float32)
        for i in range(GROUP):
            s = g * GROUP + i
            top, left = rows[s], cols[s]
            start = shift_side + left
            tile = jnp.minimum(start // 128, win_tiles - 2)
            shift = start - tile * 128
            piece = cut(win, shift_down + top, tile, 72)
            piece = pltpu.roll(piece, lax.rem(256 - shift, 256), 1)[:, :128]
            piece = jnp.concatenate([piece, pad], 0)
            high, low = split(piece)
            patch[:, i * 128 : (i + 1) * 128] = jnp.concatenate(
                [high, low, high, jnp.zeros((16, 128), jnp.bfloat16)], 0
            )
            tile = jnp.minimum(left // 128, sci_tiles - 2)
            shift = lax.rem(256 + i * STAMP_SIZE - (left - tile * 128), 256)
            inside = (lane >= i * STAMP_SIZE) & (lane < (i + 1) * STAMP_SIZE)
            sci_group = jnp.where(inside, pltpu.roll(cut(sci, top, tile, STAMP_SIZE), shift, 1)[:, :128], sci_group)
            var_group = jnp.where(inside, pltpu.roll(cut(var, top, tile, STAMP_SIZE), shift, 1)[:, :128], var_group)
        span = slice(g * STAMP_SIZE, (g + 1) * STAMP_SIZE)
        weight[span, :] = 1.0 / jnp.sqrt(var_group)
        basis[28 * 128 + g * STAMP_SIZE : 28 * 128 + (g + 1) * STAMP_SIZE, :] = sci_group
        filtered = jnp.dot(vband[...], patch[...], preferred_element_type=jnp.float32)
        for m in range(FILTERS):
            vert[m * 128 + g * 32 : m * 128 + g * 32 + 32, :] = filtered[
                m * 32 : m * 32 + 32
            ].astype(jnp.bfloat16)
    basis[27 * 128 : 28 * 128, :] = jnp.ones((128, 128), jnp.float32)
    basis[29 * 128 :, :] = jnp.zeros((3 * 128, 128), jnp.float32)
    for m, gaussian, members in filter_groups():
        width = len(members) * 128
        result = jnp.dot(
            vert[m * 128 : (m + 1) * 128, :],
            bands[gaussian][:, :width],
            preferred_element_type=jnp.float32,
        )
        for k, a in members:
            basis[k * 128 : (k + 1) * 128, :] = result[:, a * 128 : (a + 1) * 128]

    lane_row = lax.broadcasted_iota(jnp.int32, (1, 128), 1)
    total = jnp.zeros((2 * SYSTEM, SYSTEM), jnp.float32)
    contract = (((1,), (1,)), ((), ()))
    for g in range(STAMP_COUNT // GROUP):
        tops = jnp.zeros((1, 128), jnp.int32)
        lefts = jnp.zeros((1, 128), jnp.int32)
        for i in range(GROUP):
            inside = (lane_row >= i * STAMP_SIZE) & (lane_row < (i + 1) * STAMP_SIZE)
            tops = jnp.where(inside, rows[g * GROUP + i], tops)
            lefts = jnp.where(inside, cols[g * GROUP + i] - i * STAMP_SIZE, lefts)
        x = (2.0 * (lefts + lane_row).astype(jnp.float32) + 1.0 - columns) / columns
        tops = tops + row_base

        def one_row(r, carry):
            at = g * STAMP_SIZE + r
            y = (2.0 * (tops + r).astype(jnp.float32) + 1.0 - image_rows) / image_rows
            images = basis[pl.ds(at, SLOT, stride=128), :]
            images = images * weight[pl.ds(at, 1), :]
            place_at = pl.ds(pl.multiple_of(r * 128, 128), 128)
            for j, term in enumerate((None, x, y, x * x, x * y, y * y)):
                high, low = split(images if term is None else images * term)
                design[j * SLOT : (j + 1) * SLOT, place_at] = high
                design[SYSTEM + j * SLOT : SYSTEM + (j + 1) * SLOT, place_at] = low
            return carry

        lax.fori_loop(0, STAMP_SIZE, one_row, 0, unroll=4)
        total += lax.dot_general(
            design[...], design[:SYSTEM, :], contract, preferred_element_type=jnp.float32
        )
    total = jnp.concatenate([total, jnp.zeros((2 * SYSTEM, 256 - SYSTEM), jnp.float32)], 1)
    cross = jnp.concatenate([total[SYSTEM:], jnp.zeros((256 - SYSTEM, 256), jnp.float32)], 0)
    total = total[:SYSTEM] + cross[:SYSTEM] + cross.T[:SYSTEM]
    out[:SYSTEM, :] = total[:, :128]
    out[SYSTEM:, :] = total[128:, 128:]


def is_unknown(j, k):
    return k < BASES or (k == BASES and j < BACKGROUND_TERMS)


def solve_kernel(normal, out):
    sums = normal[...]
    first = sums[:SYSTEM]
    corner = jnp.concatenate([first[128:], jnp.zeros((SYSTEM - 128, 128), jnp.float32)], 0)
    other = jnp.concatenate([corner.T, sums[SYSTEM:]], 0)
    sums = jnp.concatenate([first, other], 1)
    row = lax.broadcasted_iota(jnp.int32, sums.shape, 0)
    col = lax.broadcasted_iota(jnp.int32, sums.shape, 1)
    slot = row % SLOT
    used = (slot < BASES) | ((slot == BASES) & (row < SLOT * BACKGROUND_TERMS))
    system = jnp.where(used, sums, 0.0)
    diagonal = used & (row == col)
    trace = jnp.sum(jnp.where(diagonal, system, 0.0), axis=(0, 1), keepdims=True)
    system = system + jnp.where(diagonal, RIDGE * trace / UNKNOWNS, 0.0)
    local = lax.broadcasted_iota(jnp.int32, (SLOT, 1), 0)
    panels = []
    for j in range(SPATIAL_TERMS):
        panel = system[:SLOT]
        count = sum(is_unknown(j, k) for k in range(SLOT))
        for k in range(0, count - 1, 2):
            at = j * SLOT + k
            row0, row1 = panel[k : k + 1], panel[k + 1 : k + 2]
            col0, col1 = panel[:, at : at + 1], panel[:, at + 1 : at + 2]
            a, b = row0[:, at : at + 1], row0[:, at + 1 : at + 2]
            c, d = row1[:, at : at + 1], row1[:, at + 1 : at + 2]
            scale = 1.0 / (a * d - b * c)
            new0 = (d * scale) * row0 - (b * scale) * row1
            new1 = (a * scale) * row1 - (c * scale) * row0
            panel = panel - col0 * new0 - col1 * new1
            panel = jnp.where(local == k, new0, jnp.where(local == k + 1, new1, panel))
        if count % 2:
            k = count - 1
            at = j * SLOT + k
            pivot_row = panel[k : k + 1] * (1.0 / panel[k : k + 1, at : at + 1])
            panel = jnp.where(local == k, pivot_row, panel - panel[:, at : at + 1] * pivot_row)
        panels.append(panel)
        if j < SPATIAL_TERMS - 1:
            below = system[SLOT:]
            system = below - jnp.dot(
                below[:, j * SLOT : (j + 1) * SLOT],
                panel,
                precision=lax.Precision.HIGHEST,
                preferred_element_type=jnp.float32,
            )
    solved = [None] * SPATIAL_TERMS
    for j in reversed(range(SPATIAL_TERMS)):
        value = panels[j][:, :128]
        for later in range(j + 1, SPATIAL_TERMS):
            value = value - jnp.dot(
                panels[j][:, later * SLOT : (later + 1) * SLOT],
                solved[later],
                precision=lax.Precision.HIGHEST,
                preferred_element_type=jnp.float32,
            )
        solved[j] = value
        out[j * SLOT : (j + 1) * SLOT, :] = value


def gather_kernel(axis_size, strip_rows, template, out, send_sem, recv_sem, pass_sem, land_sem, own_sem):
    me = lax.axis_index("exp")
    sibling = me + 1 - 2 * lax.rem(me, 2)
    hops = axis_size // 2
    first_row = pl.multiple_of(lax.axis_index("strip") * strip_rows, 8)
    own = template.at[pl.ds(first_row, out.shape[1]), :]
    peers = [lax.rem(me + 2 * h, axis_size) for h in range(1, hops)]
    barrier = pltpu.get_barrier_semaphore()
    for peer in peers + [sibling]:
        pl.semaphore_signal(barrier, inc=1, device_id={"exp": peer}, device_id_type=MESH)
    pl.semaphore_wait(barrier, hops)
    copies = []
    for h, peer in enumerate(peers + [sibling]):
        copies.append(
            pltpu.make_async_remote_copy(
                src_ref=own,
                dst_ref=out.at[me],
                send_sem=send_sem.at[h],
                recv_sem=recv_sem.at[h],
                device_id={"exp": peer},
                device_id_type=MESH,
            )
        )
        copies[-1].start()
    keep = pltpu.make_async_copy(own, out.at[me], own_sem)
    keep.start()
    passed = []
    for h in range(hops - 1):
        copies[h].wait_recv()
        source = lax.rem(me - 2 * (h + 1) + axis_size, axis_size)
        passed.append(
            pltpu.make_async_remote_copy(
                src_ref=out.at[source],
                dst_ref=out.at[source],
                send_sem=pass_sem.at[h],
                recv_sem=land_sem.at[h],
                device_id={"exp": sibling},
                device_id_type=MESH,
            )
        )
        passed[-1].start()
    copies[-1].wait_recv()
    for copy in passed:
        copy.wait_recv()
    keep.wait()
    for copy in copies + passed:
        copy.wait_send()


def vertical_kernel(
    size, sums, window, band, total, out, landed, gathered, send_sem, recv_sem, give_sem, take_sem
):
    me = lax.axis_index("strip")
    share = sums.shape[0] // size
    peers = [lax.rem(me + d, size) for d in range(1, size)]
    tiles = out.shape[1] // 256

    def one_tile(i, carry):
        at = pl.ds(pl.multiple_of(i * 256, 256), 256)
        out[:, at] = jnp.dot(
            band[...], window[:, at], preferred_element_type=jnp.float32
        ).astype(jnp.bfloat16)
        return carry

    barrier = pltpu.get_barrier_semaphore()
    for peer in peers:
        pl.semaphore_signal(barrier, inc=1, device_id={"strip": peer}, device_id_type=MESH)
    pl.semaphore_wait(barrier, size - 1)
    scattered = []
    for d, peer in enumerate(peers):
        scattered.append(
            pltpu.make_async_remote_copy(
                src_ref=sums.at[pl.ds(pl.multiple_of(peer * share, 8), share), :],
                dst_ref=landed.at[d],
                send_sem=send_sem.at[d],
                recv_sem=recv_sem.at[d],
                device_id={"strip": peer},
                device_id_type=MESH,
            )
        )
        scattered[-1].start()
    lax.fori_loop(0, tiles // 2, one_tile, 0)
    for copy in scattered:
        copy.wait_recv()
    mine = pl.ds(pl.multiple_of(me * share, 8), share)
    value = sums[mine, :]
    for d in range(size - 1):
        value = value + landed[d]
    gathered[mine, :] = value
    given = []
    for d, peer in enumerate(peers):
        given.append(
            pltpu.make_async_remote_copy(
                src_ref=gathered.at[mine, :],
                dst_ref=gathered.at[mine, :],
                send_sem=give_sem.at[d],
                recv_sem=take_sem.at[d],
                device_id={"strip": peer},
                device_id_type=MESH,
            )
        )
        given[-1].start()
    lax.fori_loop(tiles // 2, tiles, one_tile, 0)
    for copy in given:
        copy.wait_recv()
    total[...] = gathered[...]
    for copy in scattered + given:
        copy.wait_send()


def model_kernel(image_rows, columns, place, coef, sci, left, right, h0, h1, h2, out, ya, yb):
    bands = (h0, h1, h2)
    step = pl.program_id(0)
    height = sci.shape[0]
    rows = lax.broadcasted_iota(jnp.int32, (height, 128), 0) + place[2]
    y = (2.0 * rows.astype(jnp.float32) + 1.0 - image_rows) / image_rows

    @pl.when(step == 0)
    def _():
        for k in range(BASES):
            ya[k] = coef[k] + y * (coef[2 * SLOT + k] + y * coef[5 * SLOT + k])
            yb[k] = coef[SLOT + k] + y * coef[4 * SLOT + k]

    xs = []
    for t in range(MODEL_TILES):
        cols = lax.broadcasted_iota(jnp.int32, (1, 128), 1) + (step * MODEL_TILES + t) * 128
        x = (2.0 * cols.astype(jnp.float32) + 1.0 - columns) / columns
        xs.append(x)
        at = slice(t * 128, (t + 1) * 128)
        out[:, at] = sci[:, at] - (
            coef[BASES] + coef[SLOT + BASES] * x + coef[2 * SLOT + BASES] * y
        )
    for m, gaussian, members in filter_groups():
        at = slice(m * height, (m + 1) * height)
        row = jnp.concatenate([left[at, :], right[at, :]], 1)
        picture = jnp.concatenate(
            [row[:, t * 128 : t * 128 + 256] for t in range(MODEL_TILES)], 0
        )
        result = jnp.dot(
            picture, bands[gaussian][:, : len(members) * 128], preferred_element_type=jnp.float32
        )
        for t in range(MODEL_TILES):
            x = xs[t]
            part = result[t * height : (t + 1) * height]
            value = out[:, t * 128 : (t + 1) * 128]
            for k, a in members:
                field = ya[k] + x * (yb[k] + x * coef[3 * SLOT + k])
                value = value - field * part[:, a * 128 : (a + 1) * 128]
            out[:, t * 128 : (t + 1) * 128] = value


def shards(science, variance, template, offset_rows, offset_cols, stamp_rows, stamp_cols):
    strip_rows = science.shape[1]
    columns = science.shape[2]
    strip_count = lax.axis_size("strip")
    strip_index = lax.axis_index("strip")
    image_rows = strip_rows * strip_count
    window_rows = strip_rows + 2 * KERNEL_HALF
    table = filter_table()
    short = table.astype(BF16).astype(np.float32)
    row_base = strip_index * strip_rows
    exposures = lax.axis_size("exp")
    own_cols = template.shape[1]
    gather_rows = window_rows + SHIFT_MAX_ROWS
    anywhere = pl.BlockSpec(memory_space=pl.ANY)
    blocks = pl.pallas_call(
        functools.partial(gather_kernel, exposures, strip_rows),
        out_shape=jax.ShapeDtypeStruct((exposures, gather_rows, own_cols), jnp.float32),
        in_specs=[anywhere],
        out_specs=anywhere,
        scratch_shapes=[
            pltpu.SemaphoreType.DMA((exposures // 2,)),
            pltpu.SemaphoreType.DMA((exposures // 2,)),
            pltpu.SemaphoreType.DMA((max(exposures // 2 - 1, 1),)),
            pltpu.SemaphoreType.DMA((max(exposures // 2 - 1, 1),)),
            pltpu.SemaphoreType.DMA,
        ],
        compiler_params=pltpu.CompilerParams(collective_id=0, has_side_effects=True),
        name="gather",
    )(template)
    strip = blocks.transpose(1, 0, 2).reshape(gather_rows, exposures * own_cols)
    place = jnp.stack([offset_rows[0], offset_cols[0], row_base.astype(jnp.int32)])
    science = science[0]
    variance = variance[0]
    smem = pl.BlockSpec(memory_space=pltpu.SMEM)
    vmem = pl.BlockSpec(memory_space=pltpu.VMEM)
    limit = pltpu.CompilerParams(vmem_limit_bytes=56 * 1024 * 1024)
    across = [jnp.asarray(b) for b in across_bands(short)]

    normal = pl.pallas_call(
        functools.partial(stamp_kernel, image_rows, columns),
        out_shape=jax.ShapeDtypeStruct((PACKED, 128), jnp.float32),
        in_specs=[smem] * 3 + [vmem] * 7,
        out_specs=vmem,
        scratch_shapes=[
            pltpu.VMEM((256, GROUP * 128), jnp.bfloat16),
            pltpu.VMEM((FILTERS * 128, GROUP * 128), jnp.bfloat16),
            pltpu.VMEM((SLOT * 128, 128), jnp.float32),
            pltpu.VMEM((128, 128), jnp.float32),
            pltpu.VMEM((2 * SYSTEM, STAMP_SIZE * 128), jnp.bfloat16),
        ],
        compiler_params=limit,
        name="stamp_sums",
    )(
        place,
        stamp_rows[0],
        stamp_cols[0],
        strip,
        science,
        variance,
        jnp.asarray(split_band(table, STAMP_SIZE, 80, 256)),
        *[jnp.asarray(b) for b in stamp_bands(short)],
    )
    wide = -(-(columns + 128) // 256) * 256
    window = lax.dynamic_slice(
        strip, (offset_rows[0], offset_cols[0]), (window_rows, columns + 2 * KERNEL_HALF)
    )
    window = jnp.pad(window, ((0, 0), (0, wide - window.shape[1])))
    high = lax.reduce_precision(window, 8, 7)
    low = window - high
    depth = -(-3 * window_rows // 256) * 256
    filler = jnp.zeros((depth - 3 * window_rows, wide), jnp.float32)
    share = PACKED // strip_count
    copies = (strip_count - 1,)
    normal, vertical = pl.pallas_call(
        functools.partial(vertical_kernel, strip_count),
        out_shape=(
            jax.ShapeDtypeStruct((PACKED, 128), jnp.float32),
            jax.ShapeDtypeStruct((FILTERS * strip_rows, wide), jnp.bfloat16),
        ),
        in_specs=[vmem] * 3,
        out_specs=(vmem, vmem),
        scratch_shapes=[
            pltpu.VMEM((strip_count - 1, share, 128), jnp.float32),
            pltpu.VMEM((PACKED, 128), jnp.float32),
            pltpu.SemaphoreType.DMA(copies),
            pltpu.SemaphoreType.DMA(copies),
            pltpu.SemaphoreType.DMA(copies),
            pltpu.SemaphoreType.DMA(copies),
        ],
        compiler_params=pltpu.CompilerParams(
            vmem_limit_bytes=56 * 1024 * 1024, collective_id=1, has_side_effects=True
        ),
        name="vertical",
    )(
        normal,
        jnp.concatenate([high, low, high, filler], 0).astype(jnp.bfloat16),
        jnp.asarray(split_band(table, strip_rows, window_rows, depth)),
    )

    solved = pl.pallas_call(
        solve_kernel,
        out_shape=jax.ShapeDtypeStruct((SYSTEM, 128), jnp.float32),
        in_specs=[vmem],
        out_specs=vmem,
        compiler_params=limit,
        name="solve",
    )(normal)
    coefficients = solved[:, BASES + 1]

    rows_all = FILTERS * strip_rows
    step_cols = 128 * MODEL_TILES
    difference = pl.pallas_call(
        functools.partial(model_kernel, image_rows, columns),
        grid=(columns // step_cols,),
        out_shape=jax.ShapeDtypeStruct((strip_rows, columns), jnp.float32),
        in_specs=[
            smem,
            smem,
            pl.BlockSpec((strip_rows, step_cols), lambda i: (0, i)),
            pl.BlockSpec((rows_all, step_cols), lambda i: (0, i)),
            pl.BlockSpec((rows_all, 128), lambda i: (0, MODEL_TILES * (i + 1))),
        ]
        + [pl.BlockSpec(b.shape, lambda i: (0, 0)) for b in across],
        out_specs=pl.BlockSpec((strip_rows, step_cols), lambda i: (0, i)),
        scratch_shapes=[
            pltpu.VMEM((BASES, strip_rows, 128), jnp.float32),
            pltpu.VMEM((BASES, strip_rows, 128), jnp.float32),
        ],
        compiler_params=limit,
        name="model",
    )(place, coefficients, science, vertical, vertical, *across)
    return difference[None]


def solution(mesh):
    in_specs = (
        P("exp", "strip", None),
        P("exp", "strip", None),
        P(None, "exp"),
        P("exp"),
        P("exp"),
        P("exp", "strip"),
        P("exp", "strip"),
    )
    out_specs = P("exp", "strip", None)
    return jax.shard_map(shards, mesh=mesh, in_specs=in_specs, out_specs=out_specs, check_vma=False)
```

```python
import functools

import jax
import jax.numpy as jnp
import ml_dtypes
import numpy as np
from jax import lax
from jax.experimental import pallas as pl
from jax.experimental.pallas import tpu as pltpu
from jax.sharding import PartitionSpec as P

STAMP_SIZE = 32
STAMP_COUNT = 16
BASES = 27
SPATIAL_TERMS = 6
BACKGROUND_TERMS = 3
KERNEL_HALF = 20
TAPS = 2 * KERNEL_HALF + 1
UNKNOWNS = 165
SHIFT_MAX_ROWS = 24

SIGMAS = (1.0, 2.0, 4.0)
DEGREES = (4, 2, 2)
RIDGE = 0.001

SLOT = 32
SYSTEM = SLOT * SPATIAL_TERMS
FILTERS = 11
PACKED = SYSTEM + SYSTEM - 128
GROUP = 4
MODEL_TILES = 4
MESH = pl.DeviceIdType.MESH
BF16 = ml_dtypes.bfloat16


def filter_table():
    offsets = np.arange(-KERNEL_HALF, KERNEL_HALF + 1).astype(np.float64)
    entries = []
    for spread, degree in zip(SIGMAS, DEGREES):
        profile = np.exp(-offsets * offsets / (2.0 * spread * spread))
        profile = profile / np.sum(profile)
        for exponent in range(degree + 1):
            entries.append((offsets / spread) ** exponent * profile)
    return np.stack(entries).astype(np.float32)


def filter_groups():
    groups = []
    first_filter = 0
    basis = 0
    for gaussian, degree in enumerate(DEGREES):
        members = [[] for _ in range(degree + 1)]
        for across in range(degree + 1):
            for down in range(degree + 1 - across):
                members[down].append((basis, across))
                basis += 1
        for down in range(degree + 1):
            groups.append((first_filter + down, gaussian, members[down]))
        first_filter += degree + 1
    return groups


def split_band(table, out_rows, in_rows, depth):
    band = np.zeros((table.shape[0], out_rows, in_rows), np.float32)
    for r in range(out_rows):
        band[:, r, r : r + TAPS] = table
    high = band.astype(BF16)
    low = (band - high.astype(np.float32)).astype(BF16)
    full = np.zeros((table.shape[0], out_rows, depth), BF16)
    full[:, :, 0:in_rows] = high
    full[:, :, in_rows : 2 * in_rows] = high
    full[:, :, 2 * in_rows : 3 * in_rows] = low
    return full.reshape(table.shape[0] * out_rows, depth)


def stamp_bands(table):
    result = []
    first = 0
    for degree in DEGREES:
        band = np.zeros((GROUP * 128, (degree + 1) * 128), np.float32)
        for a in range(degree + 1):
            for s in range(GROUP):
                for c in range(STAMP_SIZE):
                    band[s * 128 + c : s * 128 + c + TAPS, a * 128 + s * 32 + c] = table[first + a]
        result.append(band.astype(BF16))
        first += degree + 1
    return result


def across_bands(table):
    result = []
    first = 0
    for degree in DEGREES:
        band = np.zeros((256, (degree + 1) * 128), np.float32)
        for a in range(degree + 1):
            for c in range(128):
                band[c : c + TAPS, a * 128 + c] = table[first + a]
        result.append(band.astype(BF16))
        first += degree + 1
    return result


def split(value):
    high = value.astype(jnp.bfloat16)
    low = (value - high.astype(jnp.float32)).astype(jnp.bfloat16)
    return high, low


def cut(source, top, tile, height):
    read = height + 8
    first = jnp.minimum(top // 8, (source.shape[0] - read) // 8) * 8
    block = source[
        pl.ds(pl.multiple_of(first, 8), read), pl.ds(pl.multiple_of(tile * 128, 128), 256)
    ]
    return pltpu.roll(block, lax.rem(read - (top - first), read), 0)[:height]


def stamp_kernel(
    image_rows, columns, place, rows, cols, win, sci, var, vband, h0, h1, h2,
    out, patch, vert, basis, weight, design,
):
    shift_down, shift_side, row_base = place[0], place[1], place[2]
    win_tiles = win.shape[1] // 128
    sci_tiles = columns // 128
    bands = (h0, h1, h2)
    pad = jnp.zeros((8, 128), jnp.float32)
    lane = lax.broadcasted_iota(jnp.int32, (STAMP_SIZE, 128), 1)
    for g in range(STAMP_COUNT // GROUP):
        sci_group = jnp.zeros((STAMP_SIZE, 128), jnp.float32)
        var_group = jnp.ones((STAMP_SIZE, 128), jnp.float32)
        for i in range(GROUP):
            s = g * GROUP + i
            top, left = rows[s], cols[s]
            start = shift_side + left
            tile = jnp.minimum(start // 128, win_tiles - 2)
            shift = start - tile * 128
            piece = cut(win, shift_down + top, tile, 72)
            piece = pltpu.roll(piece, lax.rem(256 - shift, 256), 1)[:, :128]
            piece = jnp.concatenate([piece, pad], 0)
            high, low = split(piece)
            patch[:, i * 128 : (i + 1) * 128] = jnp.concatenate(
                [high, low, high, jnp.zeros((16, 128), jnp.bfloat16)], 0
            )
            tile = jnp.minimum(left // 128, sci_tiles - 2)
            shift = lax.rem(256 + i * STAMP_SIZE - (left - tile * 128), 256)
            inside = (lane >= i * STAMP_SIZE) & (lane < (i + 1) * STAMP_SIZE)
            sci_group = jnp.where(inside, pltpu.roll(cut(sci, top, tile, STAMP_SIZE), shift, 1)[:, :128], sci_group)
            var_group = jnp.where(inside, pltpu.roll(cut(var, top, tile, STAMP_SIZE), shift, 1)[:, :128], var_group)
        span = slice(g * STAMP_SIZE, (g + 1) * STAMP_SIZE)
        weight[span, :] = 1.0 / jnp.sqrt(var_group)
        basis[28 * 128 + g * STAMP_SIZE : 28 * 128 + (g + 1) * STAMP_SIZE, :] = sci_group
        filtered = jnp.dot(vband[...], patch[...], preferred_element_type=jnp.float32)
        for m in range(FILTERS):
            vert[m * 128 + g * 32 : m * 128 + g * 32 + 32, :] = filtered[
                m * 32 : m * 32 + 32
            ].astype(jnp.bfloat16)
    basis[27 * 128 : 28 * 128, :] = jnp.ones((128, 128), jnp.float32)
    basis[29 * 128 :, :] = jnp.zeros((3 * 128, 128), jnp.float32)
    for m, gaussian, members in filter_groups():
        width = len(members) * 128
        result = jnp.dot(
            vert[m * 128 : (m + 1) * 128, :],
            bands[gaussian][:, :width],
            preferred_element_type=jnp.float32,
        )
        for k, a in members:
            basis[k * 128 : (k + 1) * 128, :] = result[:, a * 128 : (a + 1) * 128]

    lane_row = lax.broadcasted_iota(jnp.int32, (1, 128), 1)
    total = jnp.zeros((SYSTEM, SYSTEM), jnp.float32)
    contract = (((1,), (1,)), ((), ()))
    for g in range(STAMP_COUNT // GROUP):
        tops = jnp.zeros((1, 128), jnp.int32)
        lefts = jnp.zeros((1, 128), jnp.int32)
        for i in range(GROUP):
            inside = (lane_row >= i * STAMP_SIZE) & (lane_row < (i + 1) * STAMP_SIZE)
            tops = jnp.where(inside, rows[g * GROUP + i], tops)
            lefts = jnp.where(inside, cols[g * GROUP + i] - i * STAMP_SIZE, lefts)
        x = (2.0 * (lefts + lane_row).astype(jnp.float32) + 1.0 - columns) / columns
        tops = tops + row_base

        def one_row(r, carry):
            at = g * STAMP_SIZE + r
            y = (2.0 * (tops + r).astype(jnp.float32) + 1.0 - image_rows) / image_rows
            images = basis[pl.ds(at, SLOT, stride=128), :]
            images = images * weight[pl.ds(at, 1), :]
            place_at = pl.ds(pl.multiple_of(r * 128, 128), 128)
            for j, term in enumerate((None, x, y, x * x, x * y, y * y)):
                value = images if term is None else images * term
                design[j * SLOT : (j + 1) * SLOT, place_at] = value.astype(jnp.bfloat16)
            return carry

        lax.fori_loop(0, STAMP_SIZE, one_row, 0, unroll=4)
        total += lax.dot_general(
            design[...], design[...], contract, preferred_element_type=jnp.float32
        )
    total = jnp.concatenate([total, jnp.zeros((SYSTEM, 256 - SYSTEM), jnp.float32)], 1)
    out[:SYSTEM, :] = total[:, :128]
    out[SYSTEM:, :] = total[128:, 128:]


def is_unknown(j, k):
    return k < BASES or (k == BASES and j < BACKGROUND_TERMS)


def solve_kernel(normal, out):
    sums = normal[...]
    first = sums[:SYSTEM]
    corner = jnp.concatenate([first[128:], jnp.zeros((SYSTEM - 128, 128), jnp.float32)], 0)
    other = jnp.concatenate([corner.T, sums[SYSTEM:]], 0)
    sums = jnp.concatenate([first, other], 1)
    row = lax.broadcasted_iota(jnp.int32, sums.shape, 0)
    col = lax.broadcasted_iota(jnp.int32, sums.shape, 1)
    slot = row % SLOT
    used = (slot < BASES) | ((slot == BASES) & (row < SLOT * BACKGROUND_TERMS))
    system = jnp.where(used, sums, 0.0)
    diagonal = used & (row == col)
    trace = jnp.sum(jnp.where(diagonal, system, 0.0), axis=(0, 1), keepdims=True)
    system = system + jnp.where(diagonal, RIDGE * trace / UNKNOWNS, 0.0)
    local = lax.broadcasted_iota(jnp.int32, (SLOT // 8, 8, 256), 0) * 8
    local = local + lax.broadcasted_iota(jnp.int32, (SLOT // 8, 8, 256), 1)

    def twice(value):
        return jnp.concatenate([value, value], -1)

    def column(panel, at):
        return jnp.broadcast_to(panel[:, :, at : at + 1], (SLOT // 8, 8, 128))

    def line(value, k):
        return jnp.broadcast_to(value[k // 8, k % 8 : k % 8 + 1], (8, value.shape[2]))

    panels = []
    for j in range(SPATIAL_TERMS):
        panel = system[:SLOT].reshape(SLOT // 8, 8, 256)
        count = sum(is_unknown(j, k) for k in range(SLOT))
        for k in range(0, count - 1, 2):
            at = j * SLOT + k
            col0, col1 = column(panel, at), column(panel, at + 1)
            row0, row1 = line(panel, k), line(panel, k + 1)
            a, b, c, d = line(col0, k), line(col1, k), line(col0, k + 1), line(col1, k + 1)
            scale = 1.0 / (a * d - b * c)
            new0 = twice(d * scale) * row0 - twice(b * scale) * row1
            new1 = twice(a * scale) * row1 - twice(c * scale) * row0
            panel = panel - twice(col0) * new0[None] - twice(col1) * new1[None]
            panel = jnp.where(local == k, new0[None], jnp.where(local == k + 1, new1[None], panel))
        if count % 2:
            k = count - 1
            col = column(panel, j * SLOT + k)
            new = line(panel, k) * twice(1.0 / line(col, k))
            panel = jnp.where(local == k, new[None], panel - twice(col) * new[None])
        panel = panel.reshape(SLOT, 256)
        panels.append(panel)
        if j < SPATIAL_TERMS - 1:
            below = system[SLOT:]
            system = below - jnp.dot(
                below[:, j * SLOT : (j + 1) * SLOT],
                panel,
                precision=lax.Precision.HIGHEST,
                preferred_element_type=jnp.float32,
            )
    solved = [None] * SPATIAL_TERMS
    for j in reversed(range(SPATIAL_TERMS)):
        value = panels[j][:, :128]
        for later in range(j + 1, SPATIAL_TERMS):
            value = value - jnp.dot(
                panels[j][:, later * SLOT : (later + 1) * SLOT],
                solved[later],
                precision=lax.Precision.HIGHEST,
                preferred_element_type=jnp.float32,
            )
        solved[j] = value
        out[j * SLOT : (j + 1) * SLOT, :] = jnp.broadcast_to(
            value[:, BASES + 1 : BASES + 2], (SLOT, 128)
        )


def gather_kernel(axis_size, own, out, send_sem, recv_sem, pass_sem, land_sem, own_sem):
    me = lax.axis_index("exp")
    sibling = me + 1 - 2 * lax.rem(me, 2)
    hops = axis_size // 2
    peers = [lax.rem(me + 2 * h, axis_size) for h in range(1, hops)]
    barrier = pltpu.get_barrier_semaphore()
    for peer in peers + [sibling]:
        pl.semaphore_signal(barrier, inc=1, device_id={"exp": peer}, device_id_type=MESH)
    pl.semaphore_wait(barrier, hops)
    copies = []
    for h, peer in enumerate(peers + [sibling]):
        copies.append(
            pltpu.make_async_remote_copy(
                src_ref=own,
                dst_ref=out.at[me],
                send_sem=send_sem.at[h],
                recv_sem=recv_sem.at[h],
                device_id={"exp": peer},
                device_id_type=MESH,
            )
        )
        copies[-1].start()
    keep = pltpu.make_async_copy(own, out.at[me], own_sem)
    keep.start()
    passed = []
    for h in range(hops - 1):
        copies[h].wait_recv()
        source = lax.rem(me - 2 * (h + 1) + axis_size, axis_size)
        passed.append(
            pltpu.make_async_remote_copy(
                src_ref=out.at[source],
                dst_ref=out.at[source],
                send_sem=pass_sem.at[h],
                recv_sem=land_sem.at[h],
                device_id={"exp": sibling},
                device_id_type=MESH,
            )
        )
        passed[-1].start()
    copies[-1].wait_recv()
    for copy in passed:
        copy.wait_recv()
    keep.wait()
    for copy in copies + passed:
        copy.wait_send()


def vertical_kernel(
    size, sums, window, band, total, out, landed, gathered, send_sem, recv_sem, give_sem, take_sem
):
    me = lax.axis_index("strip")
    share = sums.shape[0] // size
    peers = [lax.rem(me + d, size) for d in range(1, size)]
    tiles = out.shape[1] // 256

    def one_tile(i, carry):
        at = pl.ds(pl.multiple_of(i * 256, 256), 256)
        out[:, at] = jnp.dot(
            band[...], window[:, at], preferred_element_type=jnp.float32
        ).astype(jnp.bfloat16)
        return carry

    barrier = pltpu.get_barrier_semaphore()
    for peer in peers:
        pl.semaphore_signal(barrier, inc=1, device_id={"strip": peer}, device_id_type=MESH)
    pl.semaphore_wait(barrier, size - 1)
    scattered = []
    for d, peer in enumerate(peers):
        scattered.append(
            pltpu.make_async_remote_copy(
                src_ref=sums.at[pl.ds(pl.multiple_of(peer * share, 8), share), :],
                dst_ref=landed.at[d],
                send_sem=send_sem.at[d],
                recv_sem=recv_sem.at[d],
                device_id={"strip": peer},
                device_id_type=MESH,
            )
        )
        scattered[-1].start()
    lax.fori_loop(0, tiles // 2, one_tile, 0)
    for copy in scattered:
        copy.wait_recv()
    mine = pl.ds(pl.multiple_of(me * share, 8), share)
    value = sums[mine, :]
    for d in range(size - 1):
        value = value + landed[d]
    gathered[mine, :] = value
    given = []
    for d, peer in enumerate(peers):
        given.append(
            pltpu.make_async_remote_copy(
                src_ref=gathered.at[mine, :],
                dst_ref=gathered.at[mine, :],
                send_sem=give_sem.at[d],
                recv_sem=take_sem.at[d],
                device_id={"strip": peer},
                device_id_type=MESH,
            )
        )
        given[-1].start()
    lax.fori_loop(tiles // 2, tiles, one_tile, 0)
    for copy in given:
        copy.wait_recv()
    total[...] = gathered[...]
    for copy in scattered + given:
        copy.wait_send()


def model_kernel(image_rows, columns, place, solved, sci, left, right, h0, h1, h2, out, ya, yb):
    bands = (h0, h1, h2)
    step = pl.program_id(0)
    height = sci.shape[0]
    rows = lax.broadcasted_iota(jnp.int32, (height, 128), 0) + place[2]
    y = (2.0 * rows.astype(jnp.float32) + 1.0 - image_rows) / image_rows

    def coef(j, k):
        return solved[j * SLOT + k : j * SLOT + k + 1, :]

    @pl.when(step == 0)
    def _():
        for k in range(BASES):
            ya[k] = coef(0, k) + y * (coef(2, k) + y * coef(5, k))
            yb[k] = coef(1, k) + y * coef(4, k)

    xs = []
    for t in range(MODEL_TILES):
        cols = lax.broadcasted_iota(jnp.int32, (1, 128), 1) + (step * MODEL_TILES + t) * 128
        x = (2.0 * cols.astype(jnp.float32) + 1.0 - columns) / columns
        xs.append(x)
        at = slice(t * 128, (t + 1) * 128)
        out[:, at] = sci[:, at] - (
            coef(0, BASES) + coef(1, BASES) * x + coef(2, BASES) * y
        )
    for m, gaussian, members in filter_groups():
        at = slice(m * height, (m + 1) * height)
        row = jnp.concatenate([left[at, :], right[at, :]], 1)
        picture = jnp.concatenate(
            [row[:, t * 128 : t * 128 + 256] for t in range(MODEL_TILES)], 0
        )
        result = jnp.dot(
            picture, bands[gaussian][:, : len(members) * 128], preferred_element_type=jnp.float32
        )
        for t in range(MODEL_TILES):
            x = xs[t]
            part = result[t * height : (t + 1) * height]
            value = out[:, t * 128 : (t + 1) * 128]
            for k, a in members:
                field = ya[k] + x * (yb[k] + x * coef(3, k))
                value = value - field * part[:, a * 128 : (a + 1) * 128]
            out[:, t * 128 : (t + 1) * 128] = value


def shards(science, variance, template, offset_rows, offset_cols, stamp_rows, stamp_cols):
    strip_rows = science.shape[1]
    columns = science.shape[2]
    strip_count = lax.axis_size("strip")
    strip_index = lax.axis_index("strip")
    image_rows = strip_rows * strip_count
    window_rows = strip_rows + 2 * KERNEL_HALF
    table = filter_table()
    short = table.astype(BF16).astype(np.float32)
    row_base = strip_index * strip_rows
    exposures = lax.axis_size("exp")
    own_cols = template.shape[1]
    gather_rows = window_rows + SHIFT_MAX_ROWS
    anywhere = pl.BlockSpec(memory_space=pl.ANY)
    blocks = pl.pallas_call(
        functools.partial(gather_kernel, exposures),
        out_shape=jax.ShapeDtypeStruct((exposures, own_cols, gather_rows), jnp.float32),
        in_specs=[anywhere],
        out_specs=anywhere,
        scratch_shapes=[
            pltpu.SemaphoreType.DMA((exposures // 2,)),
            pltpu.SemaphoreType.DMA((exposures // 2,)),
            pltpu.SemaphoreType.DMA((max(exposures // 2 - 1, 1),)),
            pltpu.SemaphoreType.DMA((max(exposures // 2 - 1, 1),)),
            pltpu.SemaphoreType.DMA,
        ],
        compiler_params=pltpu.CompilerParams(collective_id=0, has_side_effects=True),
        name="gather",
    )(lax.dynamic_slice_in_dim(template, row_base, gather_rows, 0).T)
    strip = blocks.reshape(exposures * own_cols, gather_rows).T
    place = jnp.stack([offset_rows[0], offset_cols[0], row_base.astype(jnp.int32)])
    science = science[0]
    variance = variance[0]
    smem = pl.BlockSpec(memory_space=pltpu.SMEM)
    vmem = pl.BlockSpec(memory_space=pltpu.VMEM)
    limit = pltpu.CompilerParams(vmem_limit_bytes=56 * 1024 * 1024)
    across = [jnp.asarray(b) for b in across_bands(short)]

    normal = pl.pallas_call(
        functools.partial(stamp_kernel, image_rows, columns),
        out_shape=jax.ShapeDtypeStruct((PACKED, 128), jnp.float32),
        in_specs=[smem] * 3 + [vmem] * 7,
        out_specs=vmem,
        scratch_shapes=[
            pltpu.VMEM((256, GROUP * 128), jnp.bfloat16),
            pltpu.VMEM((FILTERS * 128, GROUP * 128), jnp.bfloat16),
            pltpu.VMEM((SLOT * 128, 128), jnp.float32),
            pltpu.VMEM((128, 128), jnp.float32),
            pltpu.VMEM((SYSTEM, STAMP_SIZE * 128), jnp.bfloat16),
        ],
        compiler_params=limit,
        name="stamp_sums",
    )(
        place,
        stamp_rows[0],
        stamp_cols[0],
        strip,
        science,
        variance,
        jnp.asarray(split_band(table, STAMP_SIZE, 80, 256)),
        *[jnp.asarray(b) for b in stamp_bands(short)],
    )
    wide = -(-(columns + 128) // 256) * 256
    window = lax.dynamic_slice(
        strip, (offset_rows[0], offset_cols[0]), (window_rows, columns + 2 * KERNEL_HALF)
    )
    window = jnp.pad(window, ((0, 0), (0, wide - window.shape[1])))
    high = lax.reduce_precision(window, 8, 7)
    low = window - high
    depth = -(-3 * window_rows // 256) * 256
    filler = jnp.zeros((depth - 3 * window_rows, wide), jnp.float32)
    share = PACKED // strip_count
    copies = (strip_count - 1,)
    normal, vertical = pl.pallas_call(
        functools.partial(vertical_kernel, strip_count),
        out_shape=(
            jax.ShapeDtypeStruct((PACKED, 128), jnp.float32),
            jax.ShapeDtypeStruct((FILTERS * strip_rows, wide), jnp.bfloat16),
        ),
        in_specs=[vmem] * 3,
        out_specs=(vmem, vmem),
        scratch_shapes=[
            pltpu.VMEM((strip_count - 1, share, 128), jnp.float32),
            pltpu.VMEM((PACKED, 128), jnp.float32),
            pltpu.SemaphoreType.DMA(copies),
            pltpu.SemaphoreType.DMA(copies),
            pltpu.SemaphoreType.DMA(copies),
            pltpu.SemaphoreType.DMA(copies),
        ],
        compiler_params=pltpu.CompilerParams(
            vmem_limit_bytes=56 * 1024 * 1024, collective_id=1, has_side_effects=True
        ),
        name="vertical",
    )(
        normal,
        jnp.concatenate([high, low, high, filler], 0).astype(jnp.bfloat16),
        jnp.asarray(split_band(table, strip_rows, window_rows, depth)),
    )

    solved = pl.pallas_call(
        solve_kernel,
        out_shape=jax.ShapeDtypeStruct((SYSTEM, 128), jnp.float32),
        in_specs=[vmem],
        out_specs=vmem,
        compiler_params=limit,
        name="solve",
    )(normal)

    rows_all = FILTERS * strip_rows
    step_cols = 128 * MODEL_TILES
    difference = pl.pallas_call(
        functools.partial(model_kernel, image_rows, columns),
        grid=(columns // step_cols,),
        out_shape=jax.ShapeDtypeStruct((strip_rows, columns), jnp.float32),
        in_specs=[
            smem,
            pl.BlockSpec((SYSTEM, 128), lambda i: (0, 0)),
            pl.BlockSpec((strip_rows, step_cols), lambda i: (0, i)),
            pl.BlockSpec((rows_all, step_cols), lambda i: (0, i)),
            pl.BlockSpec((rows_all, 128), lambda i: (0, MODEL_TILES * (i + 1))),
        ]
        + [pl.BlockSpec(b.shape, lambda i: (0, 0)) for b in across],
        out_specs=pl.BlockSpec((strip_rows, step_cols), lambda i: (0, i)),
        scratch_shapes=[
            pltpu.VMEM((BASES, strip_rows, 128), jnp.float32),
            pltpu.VMEM((BASES, strip_rows, 128), jnp.float32),
        ],
        compiler_params=limit,
        name="model",
    )(place, solved, science, vertical, vertical, *across)
    return difference[None]


def solution(mesh):
    in_specs = (
        P("exp", "strip", None),
        P("exp", "strip", None),
        P(None, "exp"),
        P("exp"),
        P("exp"),
        P("exp", "strip"),
        P("exp", "strip"),
    )
    out_specs = P("exp", "strip", None)
    return jax.shard_map(shards, mesh=mesh, in_specs=in_specs, out_specs=out_specs, check_vma=False)
```

```python
import functools

import jax
import jax.numpy as jnp
import ml_dtypes
import numpy as np
from jax import lax
from jax.experimental import pallas as pl
from jax.experimental.pallas import tpu as pltpu
from jax.sharding import PartitionSpec as P

STAMP_SIZE = 32
STAMP_COUNT = 16
BASES = 27
SPATIAL_TERMS = 6
BACKGROUND_TERMS = 3
KERNEL_HALF = 20
TAPS = 2 * KERNEL_HALF + 1
UNKNOWNS = 165
SHIFT_MAX_ROWS = 24

SIGMAS = (1.0, 2.0, 4.0)
DEGREES = (4, 2, 2)
RIDGE = 0.001

SLOT = 32
SYSTEM = SLOT * SPATIAL_TERMS
FILTERS = 11
PACKED = SYSTEM + SYSTEM - 128
GROUP = 4
MODEL_TILES = 4
MESH = pl.DeviceIdType.MESH
BF16 = ml_dtypes.bfloat16


def filter_table():
    offsets = np.arange(-KERNEL_HALF, KERNEL_HALF + 1).astype(np.float64)
    entries = []
    for spread, degree in zip(SIGMAS, DEGREES):
        profile = np.exp(-offsets * offsets / (2.0 * spread * spread))
        profile = profile / np.sum(profile)
        for exponent in range(degree + 1):
            entries.append((offsets / spread) ** exponent * profile)
    return np.stack(entries).astype(np.float32)


def filter_groups():
    groups = []
    first_filter = 0
    basis = 0
    for gaussian, degree in enumerate(DEGREES):
        members = [[] for _ in range(degree + 1)]
        for across in range(degree + 1):
            for down in range(degree + 1 - across):
                members[down].append((basis, across))
                basis += 1
        for down in range(degree + 1):
            groups.append((first_filter + down, gaussian, members[down]))
        first_filter += degree + 1
    return groups


def split_band(table, out_rows, in_rows, depth):
    band = np.zeros((table.shape[0], out_rows, in_rows), np.float32)
    for r in range(out_rows):
        band[:, r, r : r + TAPS] = table
    high = band.astype(BF16)
    low = (band - high.astype(np.float32)).astype(BF16)
    full = np.zeros((table.shape[0], out_rows, depth), BF16)
    full[:, :, 0:in_rows] = high
    full[:, :, in_rows : 2 * in_rows] = high
    full[:, :, 2 * in_rows : 3 * in_rows] = low
    return full.reshape(table.shape[0] * out_rows, depth)


def stamp_bands(table):
    result = []
    first = 0
    for degree in DEGREES:
        band = np.zeros((GROUP * 128, (degree + 1) * 128), np.float32)
        for a in range(degree + 1):
            for s in range(GROUP):
                for c in range(STAMP_SIZE):
                    band[s * 128 + c : s * 128 + c + TAPS, a * 128 + s * 32 + c] = table[first + a]
        result.append(band.astype(BF16))
        first += degree + 1
    return result


def across_bands(table):
    result = []
    first = 0
    for degree in DEGREES:
        band = np.zeros((256, (degree + 1) * 128), np.float32)
        for a in range(degree + 1):
            for c in range(128):
                band[c : c + TAPS, a * 128 + c] = table[first + a]
        result.append(band.astype(BF16))
        first += degree + 1
    return result


def split(value):
    high = value.astype(jnp.bfloat16)
    low = (value - high.astype(jnp.float32)).astype(jnp.bfloat16)
    return high, low


def cut(source, top, tile, height):
    read = height + 8
    first = jnp.minimum(top // 8, (source.shape[0] - read) // 8) * 8
    block = source[
        pl.ds(pl.multiple_of(first, 8), read), pl.ds(pl.multiple_of(tile * 128, 128), 256)
    ]
    return pltpu.roll(block, lax.rem(read - (top - first), read), 0)[:height]


def stamp_kernel(
    image_rows, columns, place, rows, cols, win, sci, var, vband, h0, h1, h2,
    out, patch, vert, basis, weight, design,
):
    shift_down, shift_side, row_base = place[0], place[1], place[2]
    win_tiles = win.shape[1] // 128
    sci_tiles = columns // 128
    bands = (h0, h1, h2)
    pad = jnp.zeros((8, 128), jnp.float32)
    lane = lax.broadcasted_iota(jnp.int32, (STAMP_SIZE, 128), 1)
    for g in range(STAMP_COUNT // GROUP):
        sci_group = jnp.zeros((STAMP_SIZE, 128), jnp.float32)
        var_group = jnp.ones((STAMP_SIZE, 128), jnp.float32)
        for i in range(GROUP):
            s = g * GROUP + i
            top, left = rows[s], cols[s]
            start = shift_side + left
            tile = jnp.minimum(start // 128, win_tiles - 2)
            shift = start - tile * 128
            piece = cut(win, shift_down + top, tile, 72)
            piece = pltpu.roll(piece, lax.rem(256 - shift, 256), 1)[:, :128]
            piece = jnp.concatenate([piece, pad], 0)
            high, low = split(piece)
            patch[:, i * 128 : (i + 1) * 128] = jnp.concatenate(
                [high, low, high, jnp.zeros((16, 128), jnp.bfloat16)], 0
            )
            tile = jnp.minimum(left // 128, sci_tiles - 2)
            shift = lax.rem(256 + i * STAMP_SIZE - (left - tile * 128), 256)
            inside = (lane >= i * STAMP_SIZE) & (lane < (i + 1) * STAMP_SIZE)
            sci_group = jnp.where(inside, pltpu.roll(cut(sci, top, tile, STAMP_SIZE), shift, 1)[:, :128], sci_group)
            var_group = jnp.where(inside, pltpu.roll(cut(var, top, tile, STAMP_SIZE), shift, 1)[:, :128], var_group)
        span = slice(g * STAMP_SIZE, (g + 1) * STAMP_SIZE)
        weight[span, :] = 1.0 / jnp.sqrt(var_group)
        basis[28 * 128 + g * STAMP_SIZE : 28 * 128 + (g + 1) * STAMP_SIZE, :] = sci_group
        filtered = jnp.dot(vband[...], patch[...], preferred_element_type=jnp.float32)
        for m in range(FILTERS):
            vert[m * 128 + g * 32 : m * 128 + g * 32 + 32, :] = filtered[
                m * 32 : m * 32 + 32
            ].astype(jnp.bfloat16)
    basis[27 * 128 : 28 * 128, :] = jnp.ones((128, 128), jnp.float32)
    basis[29 * 128 :, :] = jnp.zeros((3 * 128, 128), jnp.float32)
    for m, gaussian, members in filter_groups():
        width = len(members) * 128
        result = jnp.dot(
            vert[m * 128 : (m + 1) * 128, :],
            bands[gaussian][:, :width],
            preferred_element_type=jnp.float32,
        )
        for k, a in members:
            basis[k * 128 : (k + 1) * 128, :] = result[:, a * 128 : (a + 1) * 128]

    lane_row = lax.broadcasted_iota(jnp.int32, (1, 128), 1)
    total = jnp.zeros((SYSTEM, SYSTEM), jnp.float32)
    contract = (((1,), (1,)), ((), ()))
    for g in range(STAMP_COUNT // GROUP):
        tops = jnp.zeros((1, 128), jnp.int32)
        lefts = jnp.zeros((1, 128), jnp.int32)
        for i in range(GROUP):
            inside = (lane_row >= i * STAMP_SIZE) & (lane_row < (i + 1) * STAMP_SIZE)
            tops = jnp.where(inside, rows[g * GROUP + i], tops)
            lefts = jnp.where(inside, cols[g * GROUP + i] - i * STAMP_SIZE, lefts)
        x = (2.0 * (lefts + lane_row).astype(jnp.float32) + 1.0 - columns) / columns
        tops = tops + row_base

        def one_row(r, carry):
            at = g * STAMP_SIZE + r
            y = (2.0 * (tops + r).astype(jnp.float32) + 1.0 - image_rows) / image_rows
            images = basis[pl.ds(at, SLOT, stride=128), :]
            images = images * weight[pl.ds(at, 1), :]
            place_at = pl.ds(pl.multiple_of(r * 128, 128), 128)
            for j, term in enumerate((None, x, y, x * x, x * y, y * y)):
                value = images if term is None else images * term
                design[j * SLOT : (j + 1) * SLOT, place_at] = value.astype(jnp.bfloat16)
            return carry

        lax.fori_loop(0, STAMP_SIZE, one_row, 0, unroll=4)
        total += lax.dot_general(
            design[...], design[...], contract, preferred_element_type=jnp.float32
        )
    total = jnp.concatenate([total, jnp.zeros((SYSTEM, 256 - SYSTEM), jnp.float32)], 1)
    out[:SYSTEM, :] = total[:, :128]
    out[SYSTEM:, :] = total[128:, 128:]


def is_unknown(j, k):
    return k < BASES or (k == BASES and j < BACKGROUND_TERMS)


def solve_kernel(normal, out):
    sums = normal[...]
    first = sums[:SYSTEM]
    corner = jnp.concatenate([first[128:], jnp.zeros((SYSTEM - 128, 128), jnp.float32)], 0)
    other = jnp.concatenate([corner.T, sums[SYSTEM:]], 0)
    sums = jnp.concatenate([first, other], 1)
    row = lax.broadcasted_iota(jnp.int32, sums.shape, 0)
    col = lax.broadcasted_iota(jnp.int32, sums.shape, 1)
    slot = row % SLOT
    used = (slot < BASES) | ((slot == BASES) & (row < SLOT * BACKGROUND_TERMS))
    system = jnp.where(used, sums, 0.0)
    diagonal = used & (row == col)
    trace = jnp.sum(jnp.where(diagonal, system, 0.0), axis=(0, 1), keepdims=True)
    system = system + jnp.where(diagonal, RIDGE * trace / UNKNOWNS, 0.0)
    local = lax.broadcasted_iota(jnp.int32, (SLOT // 8, 8, 256), 0) * 8
    local = local + lax.broadcasted_iota(jnp.int32, (SLOT // 8, 8, 256), 1)

    def twice(value):
        return jnp.concatenate([value, value], -1)

    def column(panel, at):
        return jnp.broadcast_to(panel[:, :, at : at + 1], (SLOT // 8, 8, 128))

    def line(value, k):
        return jnp.broadcast_to(value[k // 8, k % 8 : k % 8 + 1], (8, value.shape[2]))

    panels = []
    for j in range(SPATIAL_TERMS):
        panel = system[:SLOT].reshape(SLOT // 8, 8, 256)
        count = sum(is_unknown(j, k) for k in range(SLOT))
        for k in range(0, count - 1, 2):
            at = j * SLOT + k
            col0, col1 = column(panel, at), column(panel, at + 1)
            row0, row1 = line(panel, k), line(panel, k + 1)
            a, b, c, d = line(col0, k), line(col1, k), line(col0, k + 1), line(col1, k + 1)
            scale = 1.0 / (a * d - b * c)
            new0 = twice(d * scale) * row0 - twice(b * scale) * row1
            new1 = twice(a * scale) * row1 - twice(c * scale) * row0
            panel = panel - twice(col0) * new0[None] - twice(col1) * new1[None]
            panel = jnp.where(local == k, new0[None], jnp.where(local == k + 1, new1[None], panel))
        if count % 2:
            k = count - 1
            col = column(panel, j * SLOT + k)
            new = line(panel, k) * twice(1.0 / line(col, k))
            panel = jnp.where(local == k, new[None], panel - twice(col) * new[None])
        panel = panel.reshape(SLOT, 256)
        panels.append(panel)
        if j < SPATIAL_TERMS - 1:
            below = system[SLOT:]
            system = below - jnp.dot(
                below[:, j * SLOT : (j + 1) * SLOT],
                panel,
                precision=lax.Precision.HIGHEST,
                preferred_element_type=jnp.float32,
            )
    solved = [None] * SPATIAL_TERMS
    for j in reversed(range(SPATIAL_TERMS)):
        value = panels[j][:, :128]
        if j < SPATIAL_TERMS - 1:
            value = value - jnp.dot(
                panels[j][:, (j + 1) * SLOT : SYSTEM],
                jnp.concatenate(solved[j + 1 :], 0),
                precision=lax.Precision.HIGHEST,
                preferred_element_type=jnp.float32,
            )
        solved[j] = value
        out[j * SLOT : (j + 1) * SLOT, :] = jnp.broadcast_to(
            value[:, BASES + 1 : BASES + 2], (SLOT, 128)
        )


def gather_kernel(axis_size, own, out, send_sem, recv_sem, pass_sem, land_sem, own_sem):
    me = lax.axis_index("exp")
    sibling = me + 1 - 2 * lax.rem(me, 2)
    hops = axis_size // 2
    peers = [lax.rem(me + 2 * h, axis_size) for h in range(1, hops)]
    barrier = pltpu.get_barrier_semaphore()
    for peer in peers + [sibling]:
        pl.semaphore_signal(barrier, inc=1, device_id={"exp": peer}, device_id_type=MESH)
    pl.semaphore_wait(barrier, hops)
    copies = []
    for h, peer in enumerate(peers + [sibling]):
        copies.append(
            pltpu.make_async_remote_copy(
                src_ref=own,
                dst_ref=out.at[me],
                send_sem=send_sem.at[h],
                recv_sem=recv_sem.at[h],
                device_id={"exp": peer},
                device_id_type=MESH,
            )
        )
        copies[-1].start()
    keep = pltpu.make_async_copy(own, out.at[me], own_sem)
    keep.start()
    passed = []
    for h in range(hops - 1):
        copies[h].wait_recv()
        source = lax.rem(me - 2 * (h + 1) + axis_size, axis_size)
        passed.append(
            pltpu.make_async_remote_copy(
                src_ref=out.at[source],
                dst_ref=out.at[source],
                send_sem=pass_sem.at[h],
                recv_sem=land_sem.at[h],
                device_id={"exp": sibling},
                device_id_type=MESH,
            )
        )
        passed[-1].start()
    copies[-1].wait_recv()
    for copy in passed:
        copy.wait_recv()
    keep.wait()
    for copy in copies + passed:
        copy.wait_send()


def vertical_kernel(
    size, sums, window_hbm, band_hbm, total, out_hbm, landed, gathered, window, band, out,
    send_sem, recv_sem, give_sem, take_sem, in_sem, out_sem,
):
    me = lax.axis_index("strip")
    share = sums.shape[0] // size
    peers = [lax.rem(me + d, size) for d in range(1, size)]
    tiles = out.shape[1] // 256

    def one_tile(i, carry):
        at = pl.ds(pl.multiple_of(i * 256, 256), 256)
        out[:, at] = jnp.dot(
            band[...], window[:, at], preferred_element_type=jnp.float32
        ).astype(jnp.bfloat16)
        pltpu.make_async_copy(out.at[:, at], out_hbm.at[:, at], out_sem.at[i]).start()
        return carry

    def one_wait(i, carry):
        at = pl.ds(pl.multiple_of(i * 256, 256), 256)
        pltpu.make_async_copy(out.at[:, at], out_hbm.at[:, at], out_sem.at[i]).wait()
        return carry

    loads = [
        pltpu.make_async_copy(window_hbm, window, in_sem.at[0]),
        pltpu.make_async_copy(band_hbm, band, in_sem.at[1]),
    ]
    for load in loads:
        load.start()
    barrier = pltpu.get_barrier_semaphore()
    for peer in peers:
        pl.semaphore_signal(barrier, inc=1, device_id={"strip": peer}, device_id_type=MESH)
    pl.semaphore_wait(barrier, size - 1)
    scattered = []
    for d, peer in enumerate(peers):
        scattered.append(
            pltpu.make_async_remote_copy(
                src_ref=sums.at[pl.ds(pl.multiple_of(peer * share, 8), share), :],
                dst_ref=landed.at[d],
                send_sem=send_sem.at[d],
                recv_sem=recv_sem.at[d],
                device_id={"strip": peer},
                device_id_type=MESH,
            )
        )
        scattered[-1].start()
    for load in loads:
        load.wait()
    lax.fori_loop(0, tiles // 2, one_tile, 0)
    for copy in scattered:
        copy.wait_recv()
    mine = pl.ds(pl.multiple_of(me * share, 8), share)
    value = sums[mine, :]
    for d in range(size - 1):
        value = value + landed[d]
    gathered[mine, :] = value
    given = []
    for d, peer in enumerate(peers):
        given.append(
            pltpu.make_async_remote_copy(
                src_ref=gathered.at[mine, :],
                dst_ref=gathered.at[mine, :],
                send_sem=give_sem.at[d],
                recv_sem=take_sem.at[d],
                device_id={"strip": peer},
                device_id_type=MESH,
            )
        )
        given[-1].start()
    lax.fori_loop(tiles // 2, tiles, one_tile, 0)
    for copy in given:
        copy.wait_recv()
    total[...] = gathered[...]
    for copy in scattered + given:
        copy.wait_send()
    lax.fori_loop(0, tiles, one_wait, 0)


def model_kernel(image_rows, columns, place, solved, sci, left, right, h0, h1, h2, out, ya, yb):
    bands = (h0, h1, h2)
    step = pl.program_id(0)
    height = sci.shape[0]
    rows = lax.broadcasted_iota(jnp.int32, (height, 128), 0) + place[2]
    y = (2.0 * rows.astype(jnp.float32) + 1.0 - image_rows) / image_rows

    def coef(j, k):
        return solved[j * SLOT + k : j * SLOT + k + 1, :]

    @pl.when(step == 0)
    def _():
        for k in range(BASES):
            ya[k] = coef(0, k) + y * (coef(2, k) + y * coef(5, k))
            yb[k] = coef(1, k) + y * coef(4, k)

    xs = []
    for t in range(MODEL_TILES):
        cols = lax.broadcasted_iota(jnp.int32, (1, 128), 1) + (step * MODEL_TILES + t) * 128
        x = (2.0 * cols.astype(jnp.float32) + 1.0 - columns) / columns
        xs.append(x)
        at = slice(t * 128, (t + 1) * 128)
        out[:, at] = sci[:, at] - (
            coef(0, BASES) + coef(1, BASES) * x + coef(2, BASES) * y
        )
    for m, gaussian, members in filter_groups():
        at = slice(m * height, (m + 1) * height)
        row = jnp.concatenate([left[at, :], right[at, :]], 1)
        picture = jnp.concatenate(
            [row[:, t * 128 : t * 128 + 256] for t in range(MODEL_TILES)], 0
        )
        result = jnp.dot(
            picture, bands[gaussian][:, : len(members) * 128], preferred_element_type=jnp.float32
        )
        for t in range(MODEL_TILES):
            x = xs[t]
            part = result[t * height : (t + 1) * height]
            value = out[:, t * 128 : (t + 1) * 128]
            for k, a in members:
                field = ya[k] + x * (yb[k] + x * coef(3, k))
                value = value - field * part[:, a * 128 : (a + 1) * 128]
            out[:, t * 128 : (t + 1) * 128] = value


def shards(science, variance, template, offset_rows, offset_cols, stamp_rows, stamp_cols):
    strip_rows = science.shape[1]
    columns = science.shape[2]
    strip_count = lax.axis_size("strip")
    strip_index = lax.axis_index("strip")
    image_rows = strip_rows * strip_count
    window_rows = strip_rows + 2 * KERNEL_HALF
    table = filter_table()
    short = table.astype(BF16).astype(np.float32)
    row_base = strip_index * strip_rows
    exposures = lax.axis_size("exp")
    own_cols = template.shape[1]
    gather_rows = window_rows + SHIFT_MAX_ROWS
    anywhere = pl.BlockSpec(memory_space=pl.ANY)
    blocks = pl.pallas_call(
        functools.partial(gather_kernel, exposures),
        out_shape=jax.ShapeDtypeStruct((exposures, own_cols, gather_rows), jnp.float32),
        in_specs=[anywhere],
        out_specs=anywhere,
        scratch_shapes=[
            pltpu.SemaphoreType.DMA((exposures // 2,)),
            pltpu.SemaphoreType.DMA((exposures // 2,)),
            pltpu.SemaphoreType.DMA((max(exposures // 2 - 1, 1),)),
            pltpu.SemaphoreType.DMA((max(exposures // 2 - 1, 1),)),
            pltpu.SemaphoreType.DMA,
        ],
        compiler_params=pltpu.CompilerParams(collective_id=0, has_side_effects=True),
        name="gather",
    )(lax.dynamic_slice_in_dim(template, row_base, gather_rows, 0).T)
    strip = blocks.reshape(exposures * own_cols, gather_rows).T
    place = jnp.stack([offset_rows[0], offset_cols[0], row_base.astype(jnp.int32)])
    science = science[0]
    variance = variance[0]
    smem = pl.BlockSpec(memory_space=pltpu.SMEM)
    vmem = pl.BlockSpec(memory_space=pltpu.VMEM)
    limit = pltpu.CompilerParams(vmem_limit_bytes=56 * 1024 * 1024)
    across = [jnp.asarray(b) for b in across_bands(short)]

    normal = pl.pallas_call(
        functools.partial(stamp_kernel, image_rows, columns),
        out_shape=jax.ShapeDtypeStruct((PACKED, 128), jnp.float32),
        in_specs=[smem] * 3 + [vmem] * 7,
        out_specs=vmem,
        scratch_shapes=[
            pltpu.VMEM((256, GROUP * 128), jnp.bfloat16),
            pltpu.VMEM((FILTERS * 128, GROUP * 128), jnp.bfloat16),
            pltpu.VMEM((SLOT * 128, 128), jnp.float32),
            pltpu.VMEM((128, 128), jnp.float32),
            pltpu.VMEM((SYSTEM, STAMP_SIZE * 128), jnp.bfloat16),
        ],
        compiler_params=limit,
        name="stamp_sums",
    )(
        place,
        stamp_rows[0],
        stamp_cols[0],
        strip,
        science,
        variance,
        jnp.asarray(split_band(table, STAMP_SIZE, 80, 256)),
        *[jnp.asarray(b) for b in stamp_bands(short)],
    )
    wide = -(-(columns + 128) // 256) * 256
    window = lax.dynamic_slice(
        strip, (offset_rows[0], offset_cols[0]), (window_rows, columns + 2 * KERNEL_HALF)
    )
    window = jnp.pad(window, ((0, 0), (0, wide - window.shape[1])))
    high = lax.reduce_precision(window, 8, 7)
    low = window - high
    depth = -(-3 * window_rows // 256) * 256
    filler = jnp.zeros((depth - 3 * window_rows, wide), jnp.float32)
    share = PACKED // strip_count
    copies = (strip_count - 1,)
    normal, vertical = pl.pallas_call(
        functools.partial(vertical_kernel, strip_count),
        out_shape=(
            jax.ShapeDtypeStruct((PACKED, 128), jnp.float32),
            jax.ShapeDtypeStruct((FILTERS * strip_rows, wide), jnp.bfloat16),
        ),
        in_specs=[vmem, anywhere, anywhere],
        out_specs=(vmem, anywhere),
        scratch_shapes=[
            pltpu.VMEM((strip_count - 1, share, 128), jnp.float32),
            pltpu.VMEM((PACKED, 128), jnp.float32),
            pltpu.VMEM((depth, wide), jnp.bfloat16),
            pltpu.VMEM((FILTERS * strip_rows, depth), jnp.bfloat16),
            pltpu.VMEM((FILTERS * strip_rows, wide), jnp.bfloat16),
            pltpu.SemaphoreType.DMA(copies),
            pltpu.SemaphoreType.DMA(copies),
            pltpu.SemaphoreType.DMA(copies),
            pltpu.SemaphoreType.DMA(copies),
            pltpu.SemaphoreType.DMA((2,)),
            pltpu.SemaphoreType.DMA((wide // 256,)),
        ],
        compiler_params=pltpu.CompilerParams(
            vmem_limit_bytes=56 * 1024 * 1024, collective_id=1, has_side_effects=True
        ),
        name="vertical",
    )(
        normal,
        jnp.concatenate([high, low, high, filler], 0).astype(jnp.bfloat16),
        jnp.asarray(split_band(table, strip_rows, window_rows, depth)),
    )

    solved = pl.pallas_call(
        solve_kernel,
        out_shape=jax.ShapeDtypeStruct((SYSTEM, 128), jnp.float32),
        in_specs=[vmem],
        out_specs=vmem,
        compiler_params=limit,
        name="solve",
    )(normal)

    rows_all = FILTERS * strip_rows
    step_cols = 128 * MODEL_TILES
    difference = pl.pallas_call(
        functools.partial(model_kernel, image_rows, columns),
        grid=(columns // step_cols,),
        out_shape=jax.ShapeDtypeStruct((strip_rows, columns), jnp.float32),
        in_specs=[
            smem,
            pl.BlockSpec((SYSTEM, 128), lambda i: (0, 0)),
            pl.BlockSpec((strip_rows, step_cols), lambda i: (0, i)),
            pl.BlockSpec((rows_all, step_cols), lambda i: (0, i)),
            pl.BlockSpec((rows_all, 128), lambda i: (0, MODEL_TILES * (i + 1))),
        ]
        + [pl.BlockSpec(b.shape, lambda i: (0, 0)) for b in across],
        out_specs=pl.BlockSpec((strip_rows, step_cols), lambda i: (0, i)),
        scratch_shapes=[
            pltpu.VMEM((BASES, strip_rows, 128), jnp.float32),
            pltpu.VMEM((BASES, strip_rows, 128), jnp.float32),
        ],
        compiler_params=limit,
        name="model",
    )(place, solved, science, vertical, vertical, *across)
    return difference[None]


def solution(mesh):
    in_specs = (
        P("exp", "strip", None),
        P("exp", "strip", None),
        P(None, "exp"),
        P("exp"),
        P("exp"),
        P("exp", "strip"),
        P("exp", "strip"),
    )
    out_specs = P("exp", "strip", None)
    return jax.shard_map(shards, mesh=mesh, in_specs=in_specs, out_specs=out_specs, check_vma=False)
```

```python
import functools

import jax
import jax.numpy as jnp
import ml_dtypes
import numpy as np
from jax import lax
from jax.experimental import pallas as pl
from jax.experimental.pallas import tpu as pltpu
from jax.sharding import PartitionSpec as P

STAMP_SIZE = 32
STAMP_COUNT = 16
BASES = 27
SPATIAL_TERMS = 6
BACKGROUND_TERMS = 3
KERNEL_HALF = 20
TAPS = 2 * KERNEL_HALF + 1
UNKNOWNS = 165
SHIFT_MAX_ROWS = 24

SIGMAS = (1.0, 2.0, 4.0)
DEGREES = (4, 2, 2)
RIDGE = 0.001

SLOT = 32
SYSTEM = SLOT * SPATIAL_TERMS
FILTERS = 11
PACKED = SYSTEM + SYSTEM - 128
GROUP = 4
MODEL_TILES = 4
MESH = pl.DeviceIdType.MESH
BF16 = ml_dtypes.bfloat16


def filter_table():
    offsets = np.arange(-KERNEL_HALF, KERNEL_HALF + 1).astype(np.float64)
    entries = []
    for spread, degree in zip(SIGMAS, DEGREES):
        profile = np.exp(-offsets * offsets / (2.0 * spread * spread))
        profile = profile / np.sum(profile)
        for exponent in range(degree + 1):
            entries.append((offsets / spread) ** exponent * profile)
    return np.stack(entries).astype(np.float32)


def filter_groups():
    groups = []
    first_filter = 0
    basis = 0
    for gaussian, degree in enumerate(DEGREES):
        members = [[] for _ in range(degree + 1)]
        for across in range(degree + 1):
            for down in range(degree + 1 - across):
                members[down].append((basis, across))
                basis += 1
        for down in range(degree + 1):
            groups.append((first_filter + down, gaussian, members[down]))
        first_filter += degree + 1
    return groups


def split_band(table, out_rows, in_rows, depth):
    band = np.zeros((table.shape[0], out_rows, in_rows), np.float32)
    for r in range(out_rows):
        band[:, r, r : r + TAPS] = table
    high = band.astype(BF16)
    low = (band - high.astype(np.float32)).astype(BF16)
    full = np.zeros((table.shape[0], out_rows, depth), BF16)
    full[:, :, 0:in_rows] = high
    full[:, :, in_rows : 2 * in_rows] = high
    full[:, :, 2 * in_rows : 3 * in_rows] = low
    return full.reshape(table.shape[0] * out_rows, depth)


def stamp_bands(table):
    result = []
    first = 0
    for degree in DEGREES:
        band = np.zeros((GROUP * 128, (degree + 1) * 128), np.float32)
        for a in range(degree + 1):
            for s in range(GROUP):
                for c in range(STAMP_SIZE):
                    band[s * 128 + c : s * 128 + c + TAPS, a * 128 + s * 32 + c] = table[first + a]
        result.append(band.astype(BF16))
        first += degree + 1
    return result


def across_bands(table):
    result = []
    first = 0
    for degree in DEGREES:
        band = np.zeros((256, (degree + 1) * 128), np.float32)
        for a in range(degree + 1):
            for c in range(128):
                band[c : c + TAPS, a * 128 + c] = table[first + a]
        result.append(band.astype(BF16))
        first += degree + 1
    return result


def split(value):
    high = value.astype(jnp.bfloat16)
    low = (value - high.astype(jnp.float32)).astype(jnp.bfloat16)
    return high, low


def cut(source, top, tile, height):
    read = height + 8
    first = jnp.minimum(top // 8, (source.shape[0] - read) // 8) * 8
    block = source[
        pl.ds(pl.multiple_of(first, 8), read), pl.ds(pl.multiple_of(tile * 128, 128), 256)
    ]
    return pltpu.roll(block, lax.rem(read - (top - first), read), 0)[:height]


def stamp_kernel(
    image_rows, columns, place, rows, cols, win, sci, var, vband, h0, h1, h2,
    out, patch, vert, basis, weight, design,
):
    shift_down, shift_side, row_base = place[0], place[1], place[2]
    win_tiles = win.shape[1] // 128
    sci_tiles = columns // 128
    bands = (h0, h1, h2)
    pad = jnp.zeros((8, 128), jnp.float32)
    lane = lax.broadcasted_iota(jnp.int32, (STAMP_SIZE, 128), 1)
    for g in range(STAMP_COUNT // GROUP):
        sci_group = jnp.zeros((STAMP_SIZE, 128), jnp.float32)
        var_group = jnp.ones((STAMP_SIZE, 128), jnp.float32)
        for i in range(GROUP):
            s = g * GROUP + i
            top, left = rows[s], cols[s]
            start = shift_side + left
            tile = jnp.minimum(start // 128, win_tiles - 2)
            shift = start - tile * 128
            piece = cut(win, shift_down + top, tile, 72)
            piece = pltpu.roll(piece, lax.rem(256 - shift, 256), 1)[:, :128]
            piece = jnp.concatenate([piece, pad], 0)
            high, low = split(piece)
            patch[:, i * 128 : (i + 1) * 128] = jnp.concatenate(
                [high, low, high, jnp.zeros((16, 128), jnp.bfloat16)], 0
            )
            tile = jnp.minimum(left // 128, sci_tiles - 2)
            shift = lax.rem(256 + i * STAMP_SIZE - (left - tile * 128), 256)
            inside = (lane >= i * STAMP_SIZE) & (lane < (i + 1) * STAMP_SIZE)
            sci_group = jnp.where(inside, pltpu.roll(cut(sci, top, tile, STAMP_SIZE), shift, 1)[:, :128], sci_group)
            var_group = jnp.where(inside, pltpu.roll(cut(var, top, tile, STAMP_SIZE), shift, 1)[:, :128], var_group)
        span = slice(g * STAMP_SIZE, (g + 1) * STAMP_SIZE)
        weight[span, :] = 1.0 / jnp.sqrt(var_group)
        basis[28 * 128 + g * STAMP_SIZE : 28 * 128 + (g + 1) * STAMP_SIZE, :] = sci_group
        filtered = jnp.dot(vband[...], patch[...], preferred_element_type=jnp.float32)
        for m in range(FILTERS):
            vert[m * 128 + g * 32 : m * 128 + g * 32 + 32, :] = filtered[
                m * 32 : m * 32 + 32
            ].astype(jnp.bfloat16)
    basis[27 * 128 : 28 * 128, :] = jnp.ones((128, 128), jnp.float32)
    basis[29 * 128 :, :] = jnp.zeros((3 * 128, 128), jnp.float32)
    for m, gaussian, members in filter_groups():
        width = len(members) * 128
        result = jnp.dot(
            vert[m * 128 : (m + 1) * 128, :],
            bands[gaussian][:, :width],
            preferred_element_type=jnp.float32,
        )
        for k, a in members:
            basis[k * 128 : (k + 1) * 128, :] = result[:, a * 128 : (a + 1) * 128]

    lane_row = lax.broadcasted_iota(jnp.int32, (1, 128), 1)
    total = jnp.zeros((SYSTEM, SYSTEM), jnp.float32)
    contract = (((1,), (1,)), ((), ()))
    for g in range(STAMP_COUNT // GROUP):
        tops = jnp.zeros((1, 128), jnp.int32)
        lefts = jnp.zeros((1, 128), jnp.int32)
        for i in range(GROUP):
            inside = (lane_row >= i * STAMP_SIZE) & (lane_row < (i + 1) * STAMP_SIZE)
            tops = jnp.where(inside, rows[g * GROUP + i], tops)
            lefts = jnp.where(inside, cols[g * GROUP + i] - i * STAMP_SIZE, lefts)
        x = (2.0 * (lefts + lane_row).astype(jnp.float32) + 1.0 - columns) / columns
        tops = tops + row_base

        def one_row(r, carry):
            at = g * STAMP_SIZE + r
            y = (2.0 * (tops + r).astype(jnp.float32) + 1.0 - image_rows) / image_rows
            images = basis[pl.ds(at, SLOT, stride=128), :]
            images = images * weight[pl.ds(at, 1), :]
            place_at = pl.ds(pl.multiple_of(r * 128, 128), 128)
            for j, term in enumerate((None, x, y, x * x, x * y, y * y)):
                value = images if term is None else images * term
                design[j * SLOT : (j + 1) * SLOT, place_at] = value.astype(jnp.bfloat16)
            return carry

        lax.fori_loop(0, STAMP_SIZE, one_row, 0, unroll=4)
        total += lax.dot_general(
            design[...], design[...], contract, preferred_element_type=jnp.float32
        )
    total = jnp.concatenate([total, jnp.zeros((SYSTEM, 256 - SYSTEM), jnp.float32)], 1)
    out[:SYSTEM, :] = total[:, :128]
    out[SYSTEM:, :] = total[128:, 128:]


def is_unknown(j, k):
    return k < BASES or (k == BASES and j < BACKGROUND_TERMS)


def invert_two(m):
    (a, b), (c, d) = m
    scale = 1.0 / (a * d - b * c)
    return [[d * scale, -b * scale], [-c * scale, a * scale]]


def times_two(p, q):
    return [[p[i][0] * q[0][j] + p[i][1] * q[1][j] for j in range(2)] for i in range(2)]


def less_two(p, q):
    return [[p[i][j] - q[i][j] for j in range(2)] for i in range(2)]


def invert_four(m):
    p, q = [m[0][:2], m[1][:2]], [m[0][2:], m[1][2:]]
    r, s = [m[2][:2], m[3][:2]], [m[2][2:], m[3][2:]]
    p_inv = invert_two(p)
    left = times_two(r, p_inv)
    right = times_two(p_inv, q)
    s_inv = invert_two(less_two(s, times_two(r, right)))
    upper = times_two(right, s_inv)
    lower = times_two(s_inv, left)
    corner = times_two(upper, left)
    top = [[p_inv[i][j] + corner[i][j] for j in range(2)] for i in range(2)]
    return [
        top[0] + [-v for v in upper[0]],
        top[1] + [-v for v in upper[1]],
        [-v for v in lower[0]] + s_inv[0],
        [-v for v in lower[1]] + s_inv[1],
    ]


def solve_kernel(normal, out):
    sums = normal[...]
    first = sums[:SYSTEM]
    corner = jnp.concatenate([first[128:], jnp.zeros((SYSTEM - 128, 128), jnp.float32)], 0)
    other = jnp.concatenate([corner.T, sums[SYSTEM:]], 0)
    sums = jnp.concatenate([first, other], 1)
    row = lax.broadcasted_iota(jnp.int32, sums.shape, 0)
    col = lax.broadcasted_iota(jnp.int32, sums.shape, 1)
    slot = row % SLOT
    used = (slot < BASES) | ((slot == BASES) & (row < SLOT * BACKGROUND_TERMS))
    system = jnp.where(used, sums, 0.0)
    diagonal = used & (row == col)
    trace = jnp.sum(jnp.where(diagonal, system, 0.0), axis=(0, 1), keepdims=True)
    system = system + jnp.where(diagonal, RIDGE * trace / UNKNOWNS, 0.0)
    local = lax.broadcasted_iota(jnp.int32, (SLOT // 8, 8, 256), 0) * 8
    local = local + lax.broadcasted_iota(jnp.int32, (SLOT // 8, 8, 256), 1)

    def twice(value):
        return jnp.concatenate([value, value], -1)

    def column(panel, at):
        return jnp.broadcast_to(panel[:, :, at : at + 1], (SLOT // 8, 8, 128))

    def line(value, k):
        return jnp.broadcast_to(value[k // 8, k % 8 : k % 8 + 1], (8, value.shape[2]))

    panels = []
    for j in range(SPATIAL_TERMS):
        panel = system[:SLOT].reshape(SLOT // 8, 8, 256)
        count = sum(is_unknown(j, k) for k in range(SLOT))
        quads = count // 4 * 4
        for k in range(0, quads, 4):
            at = j * SLOT + k
            cols = [column(panel, at + i) for i in range(4)]
            rows = [line(panel, k + i) for i in range(4)]
            entry = [[line(cols[m], k + i) for m in range(4)] for i in range(4)]
            inverse = invert_four(entry)
            news = []
            for i in range(4):
                new = twice(inverse[i][0]) * rows[0]
                for m in range(1, 4):
                    new = new + twice(inverse[i][m]) * rows[m]
                news.append(new)
            for i in range(4):
                panel = panel - twice(cols[i]) * news[i][None]
            for i in range(4):
                panel = jnp.where(local == k + i, news[i][None], panel)
        for k in range(quads, count - 1, 2):
            at = j * SLOT + k
            col0, col1 = column(panel, at), column(panel, at + 1)
            row0, row1 = line(panel, k), line(panel, k + 1)
            a, b, c, d = line(col0, k), line(col1, k), line(col0, k + 1), line(col1, k + 1)
            scale = 1.0 / (a * d - b * c)
            new0 = twice(d * scale) * row0 - twice(b * scale) * row1
            new1 = twice(a * scale) * row1 - twice(c * scale) * row0
            panel = panel - twice(col0) * new0[None] - twice(col1) * new1[None]
            panel = jnp.where(local == k, new0[None], jnp.where(local == k + 1, new1[None], panel))
        if count % 2:
            k = count - 1
            col = column(panel, j * SLOT + k)
            new = line(panel, k) * twice(1.0 / line(col, k))
            panel = jnp.where(local == k, new[None], panel - twice(col) * new[None])
        panel = panel.reshape(SLOT, 256)
        panels.append(panel)
        if j < SPATIAL_TERMS - 1:
            below = system[SLOT:]
            system = below - jnp.dot(
                below[:, j * SLOT : (j + 1) * SLOT],
                panel,
                precision=lax.Precision.HIGHEST,
                preferred_element_type=jnp.float32,
            )
    solved = [None] * SPATIAL_TERMS
    for j in reversed(range(SPATIAL_TERMS)):
        value = panels[j][:, :128]
        if j < SPATIAL_TERMS - 1:
            value = value - jnp.dot(
                panels[j][:, (j + 1) * SLOT : SYSTEM],
                jnp.concatenate(solved[j + 1 :], 0),
                precision=lax.Precision.HIGHEST,
                preferred_element_type=jnp.float32,
            )
        solved[j] = value
        out[j * SLOT : (j + 1) * SLOT, :] = jnp.broadcast_to(
            value[:, BASES + 1 : BASES + 2], (SLOT, 128)
        )


def gather_kernel(axis_size, own, out, send_sem, recv_sem, pass_sem, land_sem, own_sem):
    me = lax.axis_index("exp")
    sibling = me + 1 - 2 * lax.rem(me, 2)
    hops = axis_size // 2
    peers = [lax.rem(me + 2 * h, axis_size) for h in range(1, hops)]
    barrier = pltpu.get_barrier_semaphore()
    for peer in peers + [sibling]:
        pl.semaphore_signal(barrier, inc=1, device_id={"exp": peer}, device_id_type=MESH)
    pl.semaphore_wait(barrier, hops)
    copies = []
    for h, peer in enumerate(peers + [sibling]):
        copies.append(
            pltpu.make_async_remote_copy(
                src_ref=own,
                dst_ref=out.at[me],
                send_sem=send_sem.at[h],
                recv_sem=recv_sem.at[h],
                device_id={"exp": peer},
                device_id_type=MESH,
            )
        )
        copies[-1].start()
    keep = pltpu.make_async_copy(own, out.at[me], own_sem)
    keep.start()
    passed = []
    for h in range(hops - 1):
        copies[h].wait_recv()
        source = lax.rem(me - 2 * (h + 1) + axis_size, axis_size)
        passed.append(
            pltpu.make_async_remote_copy(
                src_ref=out.at[source],
                dst_ref=out.at[source],
                send_sem=pass_sem.at[h],
                recv_sem=land_sem.at[h],
                device_id={"exp": sibling},
                device_id_type=MESH,
            )
        )
        passed[-1].start()
    copies[-1].wait_recv()
    for copy in passed:
        copy.wait_recv()
    keep.wait()
    for copy in copies + passed:
        copy.wait_send()


def vertical_kernel(
    size, sums, window_hbm, band_hbm, total, out_hbm, landed, gathered, window, band, out,
    send_sem, recv_sem, give_sem, take_sem, in_sem, out_sem,
):
    me = lax.axis_index("strip")
    share = sums.shape[0] // size
    peers = [lax.rem(me + d, size) for d in range(1, size)]
    tiles = out.shape[1] // 256

    def one_tile(i, carry):
        at = pl.ds(pl.multiple_of(i * 256, 256), 256)
        out[:, at] = jnp.dot(
            band[...], window[:, at], preferred_element_type=jnp.float32
        ).astype(jnp.bfloat16)
        pltpu.make_async_copy(out.at[:, at], out_hbm.at[:, at], out_sem.at[i]).start()
        return carry

    def one_wait(i, carry):
        at = pl.ds(pl.multiple_of(i * 256, 256), 256)
        pltpu.make_async_copy(out.at[:, at], out_hbm.at[:, at], out_sem.at[i]).wait()
        return carry

    loads = [
        pltpu.make_async_copy(window_hbm, window, in_sem.at[0]),
        pltpu.make_async_copy(band_hbm, band, in_sem.at[1]),
    ]
    for load in loads:
        load.start()
    barrier = pltpu.get_barrier_semaphore()
    for peer in peers:
        pl.semaphore_signal(barrier, inc=1, device_id={"strip": peer}, device_id_type=MESH)
    pl.semaphore_wait(barrier, size - 1)
    scattered = []
    for d, peer in enumerate(peers):
        scattered.append(
            pltpu.make_async_remote_copy(
                src_ref=sums.at[pl.ds(pl.multiple_of(peer * share, 8), share), :],
                dst_ref=landed.at[d],
                send_sem=send_sem.at[d],
                recv_sem=recv_sem.at[d],
                device_id={"strip": peer},
                device_id_type=MESH,
            )
        )
        scattered[-1].start()
    for load in loads:
        load.wait()
    lax.fori_loop(0, tiles // 2, one_tile, 0)
    for copy in scattered:
        copy.wait_recv()
    mine = pl.ds(pl.multiple_of(me * share, 8), share)
    value = sums[mine, :]
    for d in range(size - 1):
        value = value + landed[d]
    gathered[mine, :] = value
    given = []
    for d, peer in enumerate(peers):
        given.append(
            pltpu.make_async_remote_copy(
                src_ref=gathered.at[mine, :],
                dst_ref=gathered.at[mine, :],
                send_sem=give_sem.at[d],
                recv_sem=take_sem.at[d],
                device_id={"strip": peer},
                device_id_type=MESH,
            )
        )
        given[-1].start()
    lax.fori_loop(tiles // 2, tiles, one_tile, 0)
    for copy in given:
        copy.wait_recv()
    total[...] = gathered[...]
    for copy in scattered + given:
        copy.wait_send()
    lax.fori_loop(0, tiles, one_wait, 0)


def model_kernel(image_rows, columns, place, solved, sci, left, right, h0, h1, h2, out, ya, yb):
    bands = (h0, h1, h2)
    step = pl.program_id(0)
    height = sci.shape[0]
    rows = lax.broadcasted_iota(jnp.int32, (height, 128), 0) + place[2]
    y = (2.0 * rows.astype(jnp.float32) + 1.0 - image_rows) / image_rows

    def coef(j, k):
        return solved[j * SLOT + k : j * SLOT + k + 1, :]

    @pl.when(step == 0)
    def _():
        for k in range(BASES):
            ya[k] = coef(0, k) + y * (coef(2, k) + y * coef(5, k))
            yb[k] = coef(1, k) + y * coef(4, k)

    xs = []
    for t in range(MODEL_TILES):
        cols = lax.broadcasted_iota(jnp.int32, (1, 128), 1) + (step * MODEL_TILES + t) * 128
        x = (2.0 * cols.astype(jnp.float32) + 1.0 - columns) / columns
        xs.append(x)
        at = slice(t * 128, (t + 1) * 128)
        out[:, at] = sci[:, at] - (
            coef(0, BASES) + coef(1, BASES) * x + coef(2, BASES) * y
        )
    for m, gaussian, members in filter_groups():
        at = slice(m * height, (m + 1) * height)
        row = jnp.concatenate([left[at, :], right[at, :]], 1)
        picture = jnp.concatenate(
            [row[:, t * 128 : t * 128 + 256] for t in range(MODEL_TILES)], 0
        )
        result = jnp.dot(
            picture, bands[gaussian][:, : len(members) * 128], preferred_element_type=jnp.float32
        )
        for t in range(MODEL_TILES):
            x = xs[t]
            part = result[t * height : (t + 1) * height]
            value = out[:, t * 128 : (t + 1) * 128]
            for k, a in members:
                field = ya[k] + x * (yb[k] + x * coef(3, k))
                value = value - field * part[:, a * 128 : (a + 1) * 128]
            out[:, t * 128 : (t + 1) * 128] = value


def shards(science, variance, template, offset_rows, offset_cols, stamp_rows, stamp_cols):
    strip_rows = science.shape[1]
    columns = science.shape[2]
    strip_count = lax.axis_size("strip")
    strip_index = lax.axis_index("strip")
    image_rows = strip_rows * strip_count
    window_rows = strip_rows + 2 * KERNEL_HALF
    table = filter_table()
    short = table.astype(BF16).astype(np.float32)
    row_base = strip_index * strip_rows
    exposures = lax.axis_size("exp")
    own_cols = template.shape[1]
    gather_rows = window_rows + SHIFT_MAX_ROWS
    anywhere = pl.BlockSpec(memory_space=pl.ANY)
    blocks = pl.pallas_call(
        functools.partial(gather_kernel, exposures),
        out_shape=jax.ShapeDtypeStruct((exposures, own_cols, gather_rows), jnp.float32),
        in_specs=[anywhere],
        out_specs=anywhere,
        scratch_shapes=[
            pltpu.SemaphoreType.DMA((exposures // 2,)),
            pltpu.SemaphoreType.DMA((exposures // 2,)),
            pltpu.SemaphoreType.DMA((max(exposures // 2 - 1, 1),)),
            pltpu.SemaphoreType.DMA((max(exposures // 2 - 1, 1),)),
            pltpu.SemaphoreType.DMA,
        ],
        compiler_params=pltpu.CompilerParams(collective_id=0, has_side_effects=True),
        name="gather",
    )(lax.dynamic_slice_in_dim(template, row_base, gather_rows, 0).T)
    strip = blocks.reshape(exposures * own_cols, gather_rows).T
    place = jnp.stack([offset_rows[0], offset_cols[0], row_base.astype(jnp.int32)])
    science = science[0]
    variance = variance[0]
    smem = pl.BlockSpec(memory_space=pltpu.SMEM)
    vmem = pl.BlockSpec(memory_space=pltpu.VMEM)
    limit = pltpu.CompilerParams(vmem_limit_bytes=56 * 1024 * 1024)
    across = [jnp.asarray(b) for b in across_bands(short)]

    normal = pl.pallas_call(
        functools.partial(stamp_kernel, image_rows, columns),
        out_shape=jax.ShapeDtypeStruct((PACKED, 128), jnp.float32),
        in_specs=[smem] * 3 + [vmem] * 7,
        out_specs=vmem,
        scratch_shapes=[
            pltpu.VMEM((256, GROUP * 128), jnp.bfloat16),
            pltpu.VMEM((FILTERS * 128, GROUP * 128), jnp.bfloat16),
            pltpu.VMEM((SLOT * 128, 128), jnp.float32),
            pltpu.VMEM((128, 128), jnp.float32),
            pltpu.VMEM((SYSTEM, STAMP_SIZE * 128), jnp.bfloat16),
        ],
        compiler_params=limit,
        name="stamp_sums",
    )(
        place,
        stamp_rows[0],
        stamp_cols[0],
        strip,
        science,
        variance,
        jnp.asarray(split_band(table, STAMP_SIZE, 80, 256)),
        *[jnp.asarray(b) for b in stamp_bands(short)],
    )
    wide = -(-(columns + 128) // 256) * 256
    window = lax.dynamic_slice(
        strip, (offset_rows[0], offset_cols[0]), (window_rows, columns + 2 * KERNEL_HALF)
    )
    window = jnp.pad(window, ((0, 0), (0, wide - window.shape[1])))
    high = lax.reduce_precision(window, 8, 7)
    low = window - high
    depth = -(-3 * window_rows // 256) * 256
    filler = jnp.zeros((depth - 3 * window_rows, wide), jnp.float32)
    share = PACKED // strip_count
    copies = (strip_count - 1,)
    normal, vertical = pl.pallas_call(
        functools.partial(vertical_kernel, strip_count),
        out_shape=(
            jax.ShapeDtypeStruct((PACKED, 128), jnp.float32),
            jax.ShapeDtypeStruct((FILTERS * strip_rows, wide), jnp.bfloat16),
        ),
        in_specs=[vmem, anywhere, anywhere],
        out_specs=(vmem, anywhere),
        scratch_shapes=[
            pltpu.VMEM((strip_count - 1, share, 128), jnp.float32),
            pltpu.VMEM((PACKED, 128), jnp.float32),
            pltpu.VMEM((depth, wide), jnp.bfloat16),
            pltpu.VMEM((FILTERS * strip_rows, depth), jnp.bfloat16),
            pltpu.VMEM((FILTERS * strip_rows, wide), jnp.bfloat16),
            pltpu.SemaphoreType.DMA(copies),
            pltpu.SemaphoreType.DMA(copies),
            pltpu.SemaphoreType.DMA(copies),
            pltpu.SemaphoreType.DMA(copies),
            pltpu.SemaphoreType.DMA((2,)),
            pltpu.SemaphoreType.DMA((wide // 256,)),
        ],
        compiler_params=pltpu.CompilerParams(
            vmem_limit_bytes=56 * 1024 * 1024, collective_id=1, has_side_effects=True
        ),
        name="vertical",
    )(
        normal,
        jnp.concatenate([high, low, high, filler], 0).astype(jnp.bfloat16),
        jnp.asarray(split_band(table, strip_rows, window_rows, depth)),
    )

    solved = pl.pallas_call(
        solve_kernel,
        out_shape=jax.ShapeDtypeStruct((SYSTEM, 128), jnp.float32),
        in_specs=[vmem],
        out_specs=vmem,
        compiler_params=limit,
        name="solve",
    )(normal)

    rows_all = FILTERS * strip_rows
    step_cols = 128 * MODEL_TILES
    difference = pl.pallas_call(
        functools.partial(model_kernel, image_rows, columns),
        grid=(columns // step_cols,),
        out_shape=jax.ShapeDtypeStruct((strip_rows, columns), jnp.float32),
        in_specs=[
            smem,
            pl.BlockSpec((SYSTEM, 128), lambda i: (0, 0)),
            pl.BlockSpec((strip_rows, step_cols), lambda i: (0, i)),
            pl.BlockSpec((rows_all, step_cols), lambda i: (0, i)),
            pl.BlockSpec((rows_all, 128), lambda i: (0, MODEL_TILES * (i + 1))),
        ]
        + [pl.BlockSpec(b.shape, lambda i: (0, 0)) for b in across],
        out_specs=pl.BlockSpec((strip_rows, step_cols), lambda i: (0, i)),
        scratch_shapes=[
            pltpu.VMEM((BASES, strip_rows, 128), jnp.float32),
            pltpu.VMEM((BASES, strip_rows, 128), jnp.float32),
        ],
        compiler_params=limit,
        name="model",
    )(place, solved, science, vertical, vertical, *across)
    return difference[None]


def solution(mesh):
    in_specs = (
        P("exp", "strip", None),
        P("exp", "strip", None),
        P(None, "exp"),
        P("exp"),
        P("exp"),
        P("exp", "strip"),
        P("exp", "strip"),
    )
    out_specs = P("exp", "strip", None)
    return jax.shard_map(shards, mesh=mesh, in_specs=in_specs, out_specs=out_specs, check_vma=False)
```
